256 devices in a mesh: node: 16 (over z_lo, x, core), dp: 16 (over z_hi, y).
Axes of the slice: x: 4, y: 4, z: 8 (z_hi: 4, z_lo: 2; z = z_hi * 2 + z_lo), core: 2. Of those that a mesh axis runs over, the one named last changes fastest.
Arguments:
- tokens: bfloat16 [65536, 8192], P(('node', 'dp')), may hold values from -24 to 24
- norm_gain: float32 [8192], replicated, may hold values from 0.5 to 1.5
- value_weight: bfloat16 [8192, 512], P('dp'), may hold values from -0.0625 to 0.0625
- value_grads: bfloat16 [65536, 512], P(('node', 'dp')), may hold values from -48 to 48
- new_logprobs: float32 [65536], P(('node', 'dp')), may hold values from -1.2 to 1.2
- old_logprobs: float32 [65536], P(('node', 'dp')), may hold values from -1.2 to 1.2
- advantages: float32 [512], P(('node', 'dp')), may hold values from -4 to 4
- lengths: int32 [512], P(('node', 'dp')), may hold values from 1 to 128
Outputs:
- input_grads: bfloat16 [65536, 8192], P(('node', 'dp'))
- weight_grads: float32 [8192, 512], P('dp')
- gain_grads: float32 [8192], replicated
The draws below stay inside these ranges and needn't reach their ends.
All inputs are finite; a program needn't handle non-finite values.
Results may differ from the reference program's by a relative error of at most 0.0051.
Values may be sent and summed in bfloat16 or wider, within the bound.
A program may use at most 128 MiB of HBM per device.

```python
import jax
import jax.numpy as jnp
from jax import lax

D = 8192
VW = 512
SEQ = 128
SLOTS = 256
SEQS = 512
TOKENS = 65536


def plant(array, own_key, low, top_value):
    longest = array.shape.index(max(array.shape))
    spots = []
    for shift in (0, 1):
        where = [jax.random.randint(jax.random.fold_in(own_key, axis), (), 0, length) for axis, length in enumerate(array.shape)]
        where[longest] = (where[longest] + shift) % array.shape[longest]
        spots.append(tuple(where))
    return array.at[spots[0]].set(low).at[spots[1]].set(top_value)


def raised(drawn, own_key, source, target, shards_of, factor):
    owner, partner = [(jnp.arange(drawn.shape[dim]) // (drawn.shape[dim] // shards_of)).reshape([-1 if axis == dim else 1 for axis in range(drawn.ndim)]) for dim in (source, target)]
    chosen = jax.random.permutation(own_key, shards_of)[partner]
    strong = (owner == chosen) | (owner == (partner + shards_of // 2) % shards_of)
    return jnp.where(strong, factor * drawn, drawn)


def levels(key, extent, cuts, least, largest):
    def one(dim, shards_of):
        heights = jax.random.uniform(jax.random.fold_in(jax.random.fold_in(key, 6), dim), (shards_of,), jnp.float32, least / len(cuts), largest / len(cuts))
        return jnp.repeat(jnp.exp(heights), extent[dim] // shards_of).reshape((-1,) + (1,) * (len(extent) - dim - 1))

    loudness = one(*cuts[0])
    for cut in cuts[1:]:
        loudness = loudness * one(*cut)
    return loudness


def noise(stream_key, shape, width, reach, cuts=(), kind=jnp.bfloat16):
    drawn = jax.random.normal(stream_key, shape, jnp.float32) * width
    if len(cuts) > 0:
        drawn = levels(stream_key, shape, cuts, -0.22, 0.18) * drawn
    return jnp.clip(drawn, min=-reach, max=reach).astype(kind)


def gaussian_with(key, extent, width, most, pieces, heavy, held_as=jnp.bfloat16):
    array = width * jax.random.normal(key, extent, jnp.float32)
    if pieces:
        array = array * levels(key, extent, pieces, -0.22, 0.18)
    return jnp.clip(raised(array, jax.random.fold_in(key, 3), *heavy), -most, most).astype(held_as)


def setup_inputs(seed: int = 0) -> dict:
    streams_of = jax.random.split(jax.random.key(seed), 9)
    tokens = gaussian_with(streams_of[0], (TOKENS, D), 1.0, 24.0, ((0, 256),), (0, 1, 256, 6.0))
    norm_gain = jnp.clip(1.0 + 0.1 * jax.random.normal(streams_of[1], (D,), jnp.float32), 0.5, 1.5)
    value_weight = noise(streams_of[2], (D, VW), D ** -0.5, 0.0625, ((0, 16),))
    value_grads = noise(streams_of[3], (TOKENS, VW), 8.0, 48.0, ((0, 256),))
    new_logprobs = noise(streams_of[4], (TOKENS,), 0.2, 1.2, ((0, 256),), jnp.float32)
    old_logprobs = noise(streams_of[5], (TOKENS,), 0.2, 1.2, ((0, 256),), jnp.float32)
    advantages = noise(streams_of[6], (SEQS,), 1.0, 4.0, ((0, 256),), jnp.float32)
    lengths = plant(jax.random.randint(streams_of[7], (SEQS,), 1, SEQ + 1), jax.random.fold_in(streams_of[7], 1), 1, SEQ).astype(jnp.int32)
    return dict(tokens=tokens, norm_gain=norm_gain, value_weight=value_weight, value_grads=value_grads, new_logprobs=new_logprobs, old_logprobs=old_logprobs, advantages=advantages, lengths=lengths)


epsilon = 1e-06

def block_terms(tokens_block, cotan_block, norm_gain, value_weight):
    wide_tokens = tokens_block.astype(jnp.float32)
    inverse_rms = lax.rsqrt(lax.optimization_barrier(jnp.mean(wide_tokens * wide_tokens, axis=-1, keepdims=True)) + epsilon)
    normed = (wide_tokens * inverse_rms * norm_gain).astype(jnp.bfloat16)
    normed_grad = lax.dot_general(cotan_block, value_weight, (((1,), (1,)), ((), ())), preferred_element_type=jnp.float32)
    scaled_grad = norm_gain * normed_grad
    cubed = inverse_rms * inverse_rms * inverse_rms
    input_grad = inverse_rms * scaled_grad - wide_tokens * cubed * lax.optimization_barrier(jnp.mean(wide_tokens * scaled_grad, axis=-1, keepdims=True))
    gain_part = lax.optimization_barrier(jnp.sum(normed_grad * wide_tokens * inverse_rms, axis=0))
    return (normed, input_grad.astype(jnp.bfloat16), gain_part)

def reference(tokens, norm_gain, value_weight, value_grads, new_logprobs, old_logprobs, advantages, lengths):
    seq_total = lengths.shape[0]
    length_rows = jnp.broadcast_to(lengths[:, None], (seq_total, SEQ)).reshape(TOKENS)
    advantage_rows = jnp.broadcast_to(advantages[:, None], (seq_total, SEQ)).reshape(TOKENS)
    positions = jnp.arange(TOKENS, dtype=jnp.int32) % SEQ
    alive = (positions < length_rows).astype(jnp.int32)
    ratios = jnp.exp(new_logprobs - old_logprobs)
    token_weight = -advantage_rows * jnp.clip(ratios, 0.8, 1.2) / SEQ * alive.astype(jnp.float32)
    value_cotan = (token_weight[:, None] * value_grads.astype(jnp.float32)).astype(jnp.bfloat16)
    block_total = TOKENS // SLOTS

    def one_step(carry, item):
        weight_sum, gain_sum = carry
        tokens_block, cotan_block = item
        normed, input_grad, gain_part = block_terms(tokens_block, cotan_block, norm_gain, value_weight)
        weight_sum = weight_sum + jnp.einsum('rd,rv->dv', normed, cotan_block, preferred_element_type=jnp.float32)
        return ((weight_sum, gain_sum + gain_part), input_grad)
    start_carry = (jnp.zeros((D, VW), jnp.float32), jnp.zeros((D,), jnp.float32))
    (weight_grads, gain_grads), input_grads = lax.scan(one_step, start_carry, (tokens.reshape(block_total, SLOTS, D), value_cotan.reshape(block_total, SLOTS, VW)))
    return (input_grads.reshape(TOKENS, D), weight_grads, gain_grads)
```

```python
import functools

import jax
import jax.numpy as jnp
from jax import lax
from jax.experimental import pallas as pl
from jax.experimental.pallas import tpu as pltpu
from jax.sharding import PartitionSpec as P

SEQ = 128
EPS = 1e-06
K = 8
R = 128 // K
CUT = 192
MESH = pl.DeviceIdType.MESH
F32 = jnp.float32
BF16 = jnp.bfloat16


def mod(a, n):
    return lax.rem(a + 2 * n, n)


def kernel(
    tok_hbm, gain_ref, w_hbm, vg_ref, new_ref, old_ref, adv_ref, len_ref,
    ig_hbm, wg_ref, gg_ref,
    tok, wfull, ngs, nown, nsend, nrecv, cot, cot_t, cot_t_in, inv_ref, acc,
    part, xin_a, xin_b, xin_c, yin, ts, zin, wt,
    gpart, gcore, gx, gy, gz,
    lsem, ssem, rsem,
):
    node = lax.axis_index("node")
    dp = lax.axis_index("dp")
    c = lax.rem(node, 2)
    x = lax.rem(node // 2, 4)
    lo = node // 8
    h = dp // 4
    y = lax.rem(dp, 4)
    z = 2 * h + lo
    j_me = dp

    def dev(x=x, y=y, z=z, c=c):
        return (lax.rem(z, 2) * 8 + x * 2 + c, (z // 2) * 4 + y)

    sgn = 2 * lo - 1
    z_out = mod(z + sgn, 8)
    z_mate = mod(z - sgn, 8)
    d_core = dev(c=1 - c)
    d_x = {1: dev(x=mod(x + 1, 4)), -1: dev(x=mod(x - 1, 4)), 2: dev(x=mod(x + 2, 4))}
    d_y = {1: dev(y=mod(y + 1, 4)), -1: dev(y=mod(y - 1, 4)), 2: dev(y=mod(y + 2, 4))}
    d_out = dev(z=z_out)
    d_mate = dev(z=z_mate)
    d_z = {d: dev(z=mod(z + d, 8)) for d in range(1, 8)}

    barrier = pltpu.get_barrier_semaphore()
    peers = [d_core, *d_x.values(), *d_y.values(), *d_z.values()]
    for peer in peers:
        pl.semaphore_signal(barrier, inc=1, device_id=peer, device_id_type=MESH)

    loads = []
    for r in range(4):
        loads.append(pltpu.make_async_copy(
            tok_hbm.at[pl.ds(r * 64, 64)], tok.at[pl.ds(r * 64, 64)], lsem.at[r]))
    wload = pltpu.make_async_copy(w_hbm, wfull.at[j_me], lsem.at[4])
    for cp in loads:
        cp.start()
    wload.start()

    names = {}
    sent = []

    def message(name, src, dst, device):
        index = names.setdefault(name, len(names))
        return pltpu.make_async_remote_copy(
            src_ref=src, dst_ref=dst, send_sem=ssem.at[index], recv_sem=rsem.at[index],
            device_id=device, device_id_type=MESH)

    waits = {}

    def send(name, src, dst, device):
        copy = message(name, src, dst, device)
        copy.start()
        sent.append(copy)
        waits[name] = copy

    def got(name):
        waits.pop(name).wait_recv()

    row = lax.broadcasted_iota(jnp.int32, (2, SEQ), 0)
    pos = lax.broadcasted_iota(jnp.int32, (2, SEQ), 1)
    adv = jnp.where(row == 0, adv_ref[0], adv_ref[1])
    length = jnp.where(row == 0, len_ref[0], len_ref[1])
    alive = (pos < length).astype(F32)
    ratio = jnp.exp(new_ref[...] - old_ref[...])
    weight = -adv * jnp.clip(ratio, 0.8, 1.2) / SEQ * alive
    eye = lax.broadcasted_iota(jnp.int32, (SEQ, SEQ), 0) == lax.broadcasted_iota(
        jnp.int32, (SEQ, SEQ), 1)
    for s in range(2):
        column = jnp.sum(jnp.where(eye, weight[s : s + 1, :], 0.0), axis=1, keepdims=True)
        wide = column * vg_ref[pl.ds(s * SEQ, SEQ), :].astype(F32)
        cot[pl.ds(s * SEQ, SEQ), :] = wide.astype(BF16)
        cot_t[:, pl.ds(s * SEQ, SEQ)] = wide.T.astype(BF16)

    for r in range(4):
        loads[r].wait()
        rows = pl.ds(r * 64, 64)

        def squares(i, total):
            part_ = tok[rows, pl.ds(pl.multiple_of(i * 512, 512), 512)].astype(F32)
            part_ = part_ * part_
            return total + ((part_[:, :128] + part_[:, 128:256])
                            + (part_[:, 256:384] + part_[:, 384:]))

        total = lax.fori_loop(0, 16, squares, jnp.zeros((64, 128), F32), unroll=2)
        mean = jnp.sum(total, axis=1, keepdims=True) / 8192.0
        inv_ref[rows, :] = jnp.broadcast_to(lax.rsqrt(mean + EPS), (64, 128))

    def inverse():
        return inv_ref[:, 0:1]

    def norm_block(block, dst, jj):
        lanes = pl.ds(pl.multiple_of(block * 256, 256), 256)
        value = tok[:, lanes].astype(F32) * inverse() * gain_ref[pl.ds(block, 1), :]
        dst[jj] = value.astype(BF16)

    @pl.loop(0, 16)
    def _(jj):
        norm_block(2 * jj + (1 - c), nsend, jj)

    wload.wait()
    pl.semaphore_wait(barrier, len(peers))

    events = []

    def at(time, fn):
        events.append((time, len(events), fn))

    send("cot", cot_t, cot_t_in, d_core)
    for g in range(4):
        send(("n", g), nsend.at[pl.ds(4 * g, 4)], nrecv.at[pl.ds(4 * g, 4)], d_core)

    deltas = (1, -1, 2)

    def wblock(hh, yy, lo_row, count):
        return wfull.at[mod(hh, 4) * 4 + mod(yy, 4), c, pl.ds(lo_row, count)]

    core_waits = []

    def to_core(name, ref):
        send(("k", name), ref, ref, d_core)
        core_waits.append(("k", name))

    def half_rows(unit, which):
        base, count = (CUT, 256 - CUT) if unit == "B" else (0, CUT)
        return base + which * (count // 2), count // 2

    def full_rows(unit):
        return (CUT, 256 - CUT) if unit == "B" else (0, CUT)

    def y_of(unit):
        return y if unit == "B" else y + (0, -1, 1, 2)[unit]

    def dyn_block(hh, yy, base, count):
        return wfull.at[mod(hh, 4) * 4 + mod(yy, 4), c, pl.ds(pl.multiple_of(base, 16), count)]

    def spread_b(tag, hh, base, count):
        ref = dyn_block(hh, y, base, count)
        for d in deltas:
            send(("by", tag, d), ref, ref, d_y[d])

    def got_b(tag, hh, base, count):
        for d in deltas:
            got(("by", tag, d))
            to_core(("by", tag, d), dyn_block(hh, y - d, base, count))

    def t0(unit):
        base, count = full_rows(unit)
        if unit in (1, 2, 3):
            d = deltas[unit - 1]
            got(("ay", d))
            to_core(("ay", d), wblock(h, y - d, 0, CUT))
        ref = wblock(h, y_of(unit), base, count)
        send(("o1", unit), ref, ref, d_out)
        if unit == "B":
            spread_b("own", h, base, count)

    def t1(unit):
        base, count = full_rows(unit)
        got(("o1", unit))
        ref = wblock(h + sgn, y_of(unit), base, count)
        send(("m1", unit), ref, ref, d_mate)
        to_core(("o1", unit), ref)
        if unit == "B":
            spread_b("out", h + sgn, base, count)

    def t2(unit):
        base, count = full_rows(unit)
        got(("m1", unit))
        ref = wblock(h - sgn, y_of(unit), base, count)
        first, size = half_rows(unit, 1 - lo)
        part_ref = dyn_block(h - sgn, y_of(unit), first, size)
        send(("o2", unit), part_ref, part_ref, d_out)
        to_core(("m1", unit), ref)
        if unit == "B":
            spread_b("mate", h - sgn, base, count)

    def t3(unit):
        got(("o2", unit))
        first, size = half_rows(unit, lo)
        ref = dyn_block(h + 2, y_of(unit), first, size)
        send(("m2", unit), ref, ref, d_mate)
        to_core(("o2", unit), ref)
        if unit == "B":
            spread_b("far1", h + 2, first, size)

    def t4(unit):
        got(("m2", unit))
        first, size = half_rows(unit, 1 - lo)
        ref = dyn_block(h + 2, y_of(unit), first, size)
        to_core(("m2", unit), ref)
        if unit == "B":
            spread_b("far2", h + 2, first, size)

    def start_gather():
        t0(0)
        t0("B")
        ref = wblock(h, y, 0, CUT)
        for d in deltas:
            send(("ay", d), ref, ref, d_y[d])

    at(6.0, start_gather)
    for unit, times in {
        0: (None, 11, 16, 19, 22),
        "B": (None, 12.5, 17.5, 20.5, 23.5),
        1: (12, 17, 22, 25, 28),
        2: (15, 22, 27, 30, 33),
        3: (18, 27, 32, 35, 38),
    }.items():
        for step, time in zip((t0, t1, t2, t3, t4), times):
            if time is not None:
                at(time, functools.partial(step, unit))
    bases = full_rows("B")
    at(20, lambda: got_b("own", h, *bases))
    at(22.4, lambda: got_b("out", h + sgn, *bases))
    at(24, lambda: got_b("mate", h - sgn, *bases))
    at(26, lambda: got_b("far1", h + 2, *half_rows("B", lo)))
    at(27, lambda: got_b("far2", h + 2, *half_rows("B", 1 - lo)))

    def own_norm():
        @pl.loop(0, 16)
        def _(jj):
            norm_block(2 * jj + c, nown, jj)

    at(6.5, own_norm)
    M = 256
    chunk_rows = 4 * R

    def products(m):
        if m == 0:
            got("cot")
        for g in range(4):
            if m == 0:
                got(("n", g))

            @pl.loop(0, 4)
            def _(yy, g=g):
                jj = 4 * g + yy
                rows = pl.ds(m * M, M)
                value = jnp.dot(cot_t[rows, :], nown[jj], preferred_element_type=F32)
                value += jnp.dot(cot_t_in[rows, :], nrecv[jj], preferred_element_type=F32)
                value = value.astype(BF16)
                for k in range(M // chunk_rows):
                    for q in range(4):
                        first = k * chunk_rows + q * R
                        part[m * (M // chunk_rows) + k, q, yy, g] = value[first : first + R]

    at(9.0, functools.partial(products, 0))
    at(11.0, functools.partial(products, 1))

    first_half, second_half = pl.ds(0, 2), pl.ds(2, 2)

    def x_first(k):
        x2, xr, xl = mod(x + 2, 4), mod(x + 1, 4), mod(x - 1, 4)
        send(("xa", 0, k), part.at[k, x2, first_half], xin_a.at[0, k], d_x[1])
        send(("xa", 1, k), part.at[k, x2, second_half], xin_a.at[1, k], d_x[-1])
        send(("xb", 0, k), part.at[k, xr, second_half], xin_b.at[0, k], d_x[1])
        send(("xb", 1, k), part.at[k, xl, first_half], xin_b.at[1, k], d_x[-1])

    def add_into(k, q, half, *others):
        @pl.loop(0, 2)
        def _(i):
            value = part[k, q, half * 2 + i].astype(F32)
            for other in others:
                value += other[i].astype(F32)
            part[k, q, half * 2 + i] = value.astype(BF16)

    def x_relay(k):
        xr, xl = mod(x + 1, 4), mod(x - 1, 4)
        got(("xa", 0, k))
        add_into(k, xr, 0, xin_a.at[0, k])
        send(("xc", 0, k), part.at[k, xr, first_half], xin_c.at[0, k], d_x[1])
        got(("xa", 1, k))
        add_into(k, xl, 1, xin_a.at[1, k])
        send(("xc", 1, k), part.at[k, xl, second_half], xin_c.at[1, k], d_x[-1])

    def x_last(k):
        got(("xb", 0, k))
        got(("xb", 1, k))
        got(("xc", 0, k))
        add_into(k, x, 0, xin_c.at[0, k], xin_b.at[1, k])
        got(("xc", 1, k))
        add_into(k, x, 1, xin_b.at[0, k], xin_c.at[1, k])
        for i, d in enumerate(deltas):
            send(("y", d, k), part.at[k, x, mod(y + d, 4)], yin.at[k, i], d_y[d])

    def y_last(k):
        for d in deltas:
            got(("y", d, k))
        value = part[k, x, y].astype(F32)
        for i in range(3):
            value += yin[k, i].astype(F32)
        value = value.astype(BF16)
        ts[k, 0] = value[:, :, :128]
        ts[k, 1] = value[:, :, 128:]
        for d in range(1, 8):
            z_to = mod(z + d, 8)
            send(("z", d, k), ts.at[k, lax.rem(z_to, 2), z_to // 2], zin.at[k, d - 1], d_z[d])

    def z_last(k):
        for d in range(1, 8):
            got(("z", d, k))
        value = ts[k, lo, h].astype(F32)
        for d in range(7):
            value += zin[k, d].astype(F32)
        wt[k, c, lo, x] = value.astype(BF16)
        ref = wt.at[k, c, lo, x]
        for d in deltas:
            send(("gx", d, k), ref, ref, d_x[d])

    d_diag = dev(z=z_mate, c=1 - c)

    def node_share(k):
        for d in deltas:
            got(("gx", d, k))
        ref = wt.at[k, c, lo]
        send(("gc", k), ref, ref, d_core)
        send(("gm", k), ref, ref, d_mate)
        send(("gd", k), ref, ref, d_diag)

    def write_block(k):
        for n in ("gc", "gm", "gd"):
            got((n, k))
        if (k + 1) * chunk_rows % SEQ == 0:
            first = (k + 1) * chunk_rows // SEQ - 1
            count = SEQ // chunk_rows
            for cc in range(2):
                for ll in range(2):
                    value = wt[pl.ds(first * count, count), cc, ll].astype(F32)
                    value = value.reshape(SEQ, 128)
                    wg_ref[pl.ds(cc * 256 + ll * 128, 128), pl.ds(first * SEQ, SEQ)] = value.T

    period = 36.0 / K
    for k in range(K):
        at(10.0 + max(0, k - 1) * period if k < K // 2 else max(11.5, 10 + (k - 1) * period),
           functools.partial(x_first, k))
        at(10.0 + (k + 0.8) * period, functools.partial(x_relay, k))
        done = 10.0 + (k + 1.2) * period
        at(done, functools.partial(x_last, k))
        at(done + 3, functools.partial(y_last, k))
        at(done + 6, functools.partial(z_last, k))
        at(done + 8, functools.partial(node_share, k))
        at(done + 10, functools.partial(write_block, k))

    acc_zero = []

    def row_grads(unit):
        if unit == 0:
            acc[...] = jnp.zeros_like(acc)
        while core_waits:
            name = core_waits.pop(0)
            got(name)
        yb = mod(y_of(unit), 4)

        @pl.loop(0, 8)
        def _(i):
            block = ((i // 2) * 4 + yb) * 2 + lax.rem(i, 2)
            lanes = pl.ds(pl.multiple_of(block * 256, 256), 256)
            ng = lax.dot_general(
                cot[...], wfull[(i // 2) * 4 + yb, lax.rem(i, 2)], (((1,), (1,)), ((), ())),
                preferred_element_type=F32)
            ngs[block] = ng
            both = ng * tok[:, lanes].astype(F32)
            gpart[pl.ds(block, 1), :] = jnp.sum(both * inverse(), axis=0, keepdims=True)
            both = both * gain_ref[pl.ds(block, 1), :]
            acc[...] += both[:, :128] + both[:, 128:]

    for unit, time in ((0, 28.5), (1, 30.5), (2, 34.5), (3, 40)):
        at(time, functools.partial(row_grads, unit))

    stores = []

    def finish_rows(quarter):
        inv = inverse()
        coef = inv * inv * inv * (jnp.sum(acc[...], axis=1, keepdims=True) / 8192.0)

        @pl.loop(0, 8)
        def _(i):
            block = quarter * 8 + i
            lanes = pl.ds(pl.multiple_of(block * 256, 256), 256)
            value = inv * (gain_ref[pl.ds(block, 1), :] * ngs[block]) - tok[:, lanes].astype(F32) * coef
            tok[:, lanes] = value.astype(BF16)

        lanes = pl.ds(quarter * 2048, 2048)
        copy = pltpu.make_async_copy(tok.at[:, lanes], ig_hbm.at[:, lanes], lsem.at[5 + quarter])
        copy.start()
        stores.append(copy)

    for quarter in range(4):
        at(41.5 + 0.5 * quarter, functools.partial(finish_rows, quarter))

    mine = pl.ds(pl.multiple_of(16 * c, 16), 16)

    def gain_core():
        send("g", gpart, gcore, d_core)

    def gain_x():
        got("g")
        gx[x] = gpart[mine, :] + gcore[mine, :]
        for d in deltas:
            send(("ggx", d), gx.at[x], gx.at[x], d_x[d])

    def gain_y():
        for d in deltas:
            got(("ggx", d))
        gy[y] = (gx[0] + gx[1]) + (gx[2] + gx[3])
        for d in deltas:
            send(("ggy", d), gy.at[y], gy.at[y], d_y[d])

    def gain_z():
        for d in deltas:
            got(("ggy", d))
        gz[z] = (gy[0] + gy[1]) + (gy[2] + gy[3])
        for d in range(1, 8):
            send(("ggz", d), gz.at[z], gz.at[z], d_z[d])

    def gain_last():
        for d in range(1, 8):
            got(("ggz", d))
        total = gz[0]
        for i in range(1, 8):
            total += gz[i]
        gg_ref[mine, :] = total
        send("gg", gg_ref.at[mine], gg_ref.at[mine], d_core)

    at(40.1, gain_core)
    at(42.1, gain_x)
    at(44.5, gain_y)
    at(47, gain_z)
    at(50, gain_last)
    at(59, lambda: got("gg"))

    for _, _, fn in sorted(events, key=lambda e: e[:2]):
        fn()
    for copy in sent:
        copy.wait_send()
    for copy in stores:
        copy.wait()


MESSAGES = 22 * K + 5 + 3 + 20 + 15 + 38 + 15


def on_device(
    tokens, norm_gain, value_weight, value_grads, new_logprobs, old_logprobs, advantages, lengths
):
    vmem = pl.BlockSpec(memory_space=pltpu.VMEM)
    smem = pl.BlockSpec(memory_space=pltpu.SMEM)
    hbm = pl.BlockSpec(memory_space=pl.ANY)
    input_grads, weight_grads, gain_grads = pl.pallas_call(
        kernel,
        out_shape=(
            jax.ShapeDtypeStruct((256, 8192), BF16),
            jax.ShapeDtypeStruct((512, 512), F32),
            jax.ShapeDtypeStruct((32, 256), F32),
        ),
        in_specs=[hbm, vmem, hbm, vmem, vmem, vmem, smem, smem],
        out_specs=(hbm, vmem, vmem),
        scratch_shapes=[
            pltpu.VMEM((256, 8192), BF16),
            pltpu.VMEM((16, 2, 256, 512), BF16),
            pltpu.VMEM((32, 256, 256), F32),
            pltpu.VMEM((16, 256, 256), BF16),
            pltpu.VMEM((16, 256, 256), BF16),
            pltpu.VMEM((16, 256, 256), BF16),
            pltpu.VMEM((256, 512), BF16),
            pltpu.VMEM((512, 256), BF16),
            pltpu.VMEM((512, 256), BF16),
            pltpu.VMEM((256, 128), F32),
            pltpu.VMEM((256, 128), F32),
            pltpu.VMEM((K, 4, 4, 4, R, 256), BF16),
            pltpu.VMEM((2, K, 2, 4, R, 256), BF16),
            pltpu.VMEM((2, K, 2, 4, R, 256), BF16),
            pltpu.VMEM((2, K, 2, 4, R, 256), BF16),
            pltpu.VMEM((K, 3, 4, R, 256), BF16),
            pltpu.VMEM((K, 2, 4, R, 128), BF16),
            pltpu.VMEM((K, 7, R, 128), BF16),
            pltpu.VMEM((K, 2, 2, 4, R, 128), BF16),
            pltpu.VMEM((32, 256), F32),
            pltpu.VMEM((32, 256), F32),
            pltpu.VMEM((4, 16, 256), F32),
            pltpu.VMEM((4, 16, 256), F32),
            pltpu.VMEM((8, 16, 256), F32),
            pltpu.SemaphoreType.DMA((9,)),
            pltpu.SemaphoreType.DMA((MESSAGES,)),
            pltpu.SemaphoreType.DMA((MESSAGES,)),
        ],
        compiler_params=pltpu.CompilerParams(
            collective_id=0, has_side_effects=True, vmem_limit_bytes=56 * 2**20
        ),
    )(
        tokens,
        norm_gain.reshape(32, 256),
        value_weight.reshape(2, 256, 512),
        value_grads,
        new_logprobs.reshape(2, SEQ),
        old_logprobs.reshape(2, SEQ),
        advantages,
        lengths,
    )
    return input_grads, weight_grads, gain_grads.reshape(8192)


def solution(mesh):
    rows = P(("node", "dp"))
    in_specs = (
        P(("node", "dp"), None), P(), P("dp", None), P(("node", "dp"), None), rows, rows, rows, rows,
    )
    out_specs = (P(("node", "dp"), None), P("dp", None), P())
    return jax.shard_map(
        on_device, mesh=mesh, in_specs=in_specs, out_specs=out_specs, check_vma=False
    )
```

```python
import functools

import jax
import jax.numpy as jnp
from jax import lax
from jax.experimental import pallas as pl
from jax.experimental.pallas import tpu as pltpu
from jax.sharding import PartitionSpec as P

SEQ = 128
EPS = 1e-06
K = 8
R = 128 // K
YF = ()
FAST = 2
CUT = 160
ORDER = (
    ("t0", 0, 0), ("t0", 0, 1), ("t0", 4, "b"), ("p", 0, 0), ("p", 0, 1), ("p", 0, 2), ("t0", 1, 0),
    ("t0", 2, 0), ("t1", 0, 0), ("p", 0, 3), ("xf", 0), ("xf", 1), ("p", 1, 0), ("p", 1, 1), ("t1", 0, 1),
    ("p", 1, 2), ("t0", 3, 0), ("p", 1, 3), ("t0", 1, 1), ("t0", 2, 1), ("t1", 4, "b"), ("t2", 0, 0),
    ("xr", 0, 0), ("xr", 1, 0), ("xf", 2), ("t1", 1, 0), ("t0", 3, 1), ("t2", 0, 1), ("t1", 2, 0),
    ("xr", 0, 1), ("xr", 1, 1), ("xf", 3), ("t1", 3, 0), ("t2", 4, "b"), ("b", 0), ("xl", 0), ("t1", 1, 1),
    ("t2", 1, 0), ("xr", 0, 2), ("xr", 1, 2), ("xf", 4), ("t1", 2, 1), ("t2", 2, 0), ("b", 1), ("t1", 3, 1),
    ("t2", 3, 0), ("xl", 1), ("xr", 0, 3), ("xr", 1, 3), ("xf", 5), ("t3", 0), ("t2", 1, 1), ("t3", 4),
    ("t2", 2, 1), ("b", 2), ("xl", 2), ("t2", 3, 1), ("yl", 0), ("xr", 0, 4), ("xr", 1, 4), ("xf", 6),
    ("t3", 1), ("yl", 1), ("t4", 0), ("t4", 4), ("t3", 2), ("xl", 3), ("b", 3), ("rg", 0), ("xr", 0, 5),
    ("xr", 1, 5), ("t3", 3), ("xf", 7), ("t4", 1), ("yl", 2), ("zl", 0), ("xl", 4), ("b", 4), ("zl", 1),
    ("t4", 2), ("xr", 0, 6), ("xr", 1, 6), ("yl", 3), ("rg", 1), ("t4", 3), ("rg", 2), ("xl", 5),
    ("xr", 0, 7), ("xr", 1, 7), ("yl", 4), ("zl", 2), ("zl", 3), ("ns", 0), ("ns", 1), ("rg", 3), ("g", 0),
    ("xl", 6), ("fr", 0), ("xl", 7), ("g", 1), ("yl", 5), ("wr", 0), ("wr", 1), ("zl", 4), ("ns", 2),
    ("ns", 3), ("fr", 1), ("fr", 2), ("fr", 3), ("yl", 6), ("g", 2), ("yl", 7), ("ns", 4), ("wr", 2),
    ("zl", 5), ("wr", 3), ("g", 3), ("ns", 5), ("zl", 6), ("wr", 4), ("zl", 7), ("g", 4), ("wr", 5),
    ("wr", 6), ("wr", 7), ("g", 5),
)
MESH = pl.DeviceIdType.MESH
F32 = jnp.float32
BF16 = jnp.bfloat16


def mod(a, n):
    return lax.rem(a + 2 * n, n)


def kernel(
    tok_hbm, gain_ref, w_hbm, vg_ref, new_ref, old_ref, adv_ref, len_ref,
    ig_hbm, wg_ref, gg_ref,
    tok, wfull, ngs, nown, nsend, nrecv, cot, cot_t, cot_t_in, inv_ref, acc,
    part, xin_a, xin_b, xin_c, yin, ts, zin, wt, yf_in, xd_in, tsf, zinf,
    gpart, gcore, gx, gy, gz,
    lsem, ssem, rsem,
):
    node = lax.axis_index("node")
    dp = lax.axis_index("dp")
    c = lax.rem(node, 2)
    x = lax.rem(node // 2, 4)
    lo = node // 8
    h = dp // 4
    y = lax.rem(dp, 4)
    z = 2 * h + lo
    j_me = dp

    def dev(x=x, y=y, z=z, c=c):
        return (lax.rem(z, 2) * 8 + x * 2 + c, (z // 2) * 4 + y)

    sgn = 2 * lo - 1
    z_out = mod(z + sgn, 8)
    z_mate = mod(z - sgn, 8)
    d_core = dev(c=1 - c)
    d_x = {1: dev(x=mod(x + 1, 4)), -1: dev(x=mod(x - 1, 4)), 2: dev(x=mod(x + 2, 4))}
    d_y = {1: dev(y=mod(y + 1, 4)), -1: dev(y=mod(y - 1, 4)), 2: dev(y=mod(y + 2, 4))}
    d_out = dev(z=z_out)
    d_mate = dev(z=z_mate)
    d_z = {d: dev(z=mod(z + d, 8)) for d in range(1, 8)}

    d_diag = dev(z=z_mate, c=1 - c)
    d_xf = {d: dev(x=mod(x + d, 4), c=1 - c) for d in (1, -1, 2)}

    barrier = pltpu.get_barrier_semaphore()
    peers = [d_core, *d_x.values(), *d_xf.values(), *d_y.values(), *d_z.values(), d_diag]
    for peer in peers:
        pl.semaphore_signal(barrier, inc=1, device_id=peer, device_id_type=MESH)

    loads = []
    for r in range(4):
        loads.append(pltpu.make_async_copy(
            tok_hbm.at[pl.ds(r * 64, 64)], tok.at[pl.ds(r * 64, 64)], lsem.at[r]))
    wload = pltpu.make_async_copy(w_hbm, wfull.at[j_me], lsem.at[4])
    for cp in loads:
        cp.start()
    wload.start()

    names = {}
    sent = []

    def message(name, src, dst, device):
        index = names.setdefault(name, len(names))
        return pltpu.make_async_remote_copy(
            src_ref=src, dst_ref=dst, send_sem=ssem.at[index], recv_sem=rsem.at[index],
            device_id=device, device_id_type=MESH)

    waits = {}

    def send(name, src, dst, device):
        copy = message(name, src, dst, device)
        copy.start()
        sent.append(copy)
        waits[name] = copy

    def got(name):
        waits.pop(name).wait_recv()

    row = lax.broadcasted_iota(jnp.int32, (2, SEQ), 0)
    pos = lax.broadcasted_iota(jnp.int32, (2, SEQ), 1)
    adv = jnp.where(row == 0, adv_ref[0], adv_ref[1])
    length = jnp.where(row == 0, len_ref[0], len_ref[1])
    alive = (pos < length).astype(F32)
    ratio = jnp.exp(new_ref[...] - old_ref[...])
    weight = -adv * jnp.clip(ratio, 0.8, 1.2) / SEQ * alive
    eye = lax.broadcasted_iota(jnp.int32, (SEQ, SEQ), 0) == lax.broadcasted_iota(
        jnp.int32, (SEQ, SEQ), 1)
    for s in range(2):
        column = jnp.sum(jnp.where(eye, weight[s : s + 1, :], 0.0), axis=1, keepdims=True)
        wide = column * vg_ref[pl.ds(s * SEQ, SEQ), :].astype(F32)
        cot[pl.ds(s * SEQ, SEQ), :] = wide.astype(BF16)
        cot_t[:, pl.ds(s * SEQ, SEQ)] = wide.T.astype(BF16)

    for r in range(4):
        loads[r].wait()
        rows = pl.ds(r * 64, 64)

        def squares(i, total):
            part_ = tok[rows, pl.ds(pl.multiple_of(i * 512, 512), 512)].astype(F32)
            part_ = part_ * part_
            return total + ((part_[:, :128] + part_[:, 128:256])
                            + (part_[:, 256:384] + part_[:, 384:]))

        total = lax.fori_loop(0, 16, squares, jnp.zeros((64, 128), F32), unroll=2)
        mean = jnp.sum(total, axis=1, keepdims=True) / 8192.0
        inv_ref[rows, :] = jnp.broadcast_to(lax.rsqrt(mean + EPS), (64, 128))

    def inverse():
        return inv_ref[:, 0:1]

    def gain_row(block):
        return jnp.concatenate([gain_ref[pl.ds(2 * block, 1), :], gain_ref[pl.ds(2 * block + 1, 1), :]], axis=1)

    def norm_block(block, dst, jj):
        lanes = pl.ds(pl.multiple_of(block * 256, 256), 256)
        value = tok[:, lanes].astype(F32) * inverse() * gain_row(block)
        dst[jj] = value.astype(BF16)

    @pl.loop(0, 16)
    def _(jj):
        norm_block(2 * jj + (1 - c), nsend, jj)

    @pl.loop(0, 16)
    def _(jj):
        norm_block(2 * jj + c, nown, jj)

    wload.wait()
    pl.semaphore_wait(barrier, len(peers))

    events = {}

    def piece(name, fn, *args):
        events[name] = functools.partial(fn, *args)

    send("cot", cot_t, cot_t_in, d_core)
    for g in range(4):
        send(("n", g), nsend.at[pl.ds(4 * g, 4)], nrecv.at[pl.ds(4 * g, 4)], d_core)

    deltas = (1, -1, 2)

    from_core = {0: [], 1: [], 2: [], 3: []}

    def to_core(name, ref, group):
        send(("k", name), ref, ref, d_core)
        from_core[group].append(("k", name))

    def rows_of(unit):
        if unit[1] == "b":
            return CUT, 256 - CUT
        return unit[1] * (CUT // 2), CUT // 2

    def half_rows(u, which):
        if u == 4:
            return CUT + which * ((256 - CUT) // 2), (256 - CUT) // 2
        return which * (CUT // 2), CUT // 2

    def y_of(u):
        return y + (0, -1, 1, 2, 0)[u]

    def block_rows(hh, yy, base, count):
        return wfull.at[mod(hh, 4) * 4 + mod(yy, 4), c, pl.ds(pl.multiple_of(base, 16), count)]

    def group_of(u):
        return u % 4

    def spread_b(tag, hh, base, count):
        ref = block_rows(hh, y, base, count)
        for d in deltas:
            send(("by", tag, d), ref, ref, d_y[d])

    def got_b(tag, hh, base, count):
        for i, d in enumerate(deltas):
            got(("by", tag, d))
            to_core(("by", tag, d), block_rows(hh, y - d, base, count), i + 1)

    def t0(unit):
        u, s = unit
        base, count = rows_of(unit)
        if u in (1, 2, 3):
            d = deltas[u - 1]
            got(("ay", d, s))
            to_core(("ay", d, s), block_rows(h, y - d, base, count), u)
        ref = block_rows(h, y_of(u), base, count)
        send(("o1", unit), ref, ref, d_out)
        if u == 4:
            spread_b("own", h, base, count)
        elif u == 0:
            for d in deltas:
                send(("ay", d, s), ref, ref, d_y[d])

    def t1(unit):
        u = unit[0]
        base, count = rows_of(unit)
        got(("o1", unit))
        ref = block_rows(h + sgn, y_of(u), base, count)
        send(("m1", unit), ref, ref, d_mate)
        to_core(("o1", unit), ref, group_of(u))
        if u == 4:
            spread_b("out", h + sgn, base, count)

    def t2(unit):
        u, s = unit
        base, count = rows_of(unit)
        got(("m1", unit))
        ref = block_rows(h - sgn, y_of(u), base, count)
        if s != 0:
            half = block_rows(h - sgn, y_of(u), *half_rows(u, 1 - lo))
            send(("o2", u), half, half, d_out)
        to_core(("m1", unit), ref, group_of(u))
        if u == 4:
            spread_b("mate", h - sgn, base, count)

    def t3(u):
        got(("o2", u))
        first, size = half_rows(u, lo)
        ref = block_rows(h + 2, y_of(u), first, size)
        send(("m2", u), ref, ref, d_mate)
        to_core(("o2", u), ref, group_of(u))
        if u == 4:
            spread_b("far1", h + 2, first, size)

    def t4(u):
        got(("m2", u))
        first, size = half_rows(u, 1 - lo)
        ref = block_rows(h + 2, y_of(u), first, size)
        to_core(("m2", u), ref, group_of(u))
        if u == 4:
            spread_b("far2", h + 2, first, size)

    for u in range(5):
        for s in ((0, 1) if u < 4 else ("b",)):
            piece(("t0", u, s), t0, (u, s))
            piece(("t1", u, s), t1, (u, s))
            piece(("t2", u, s), t2, (u, s))
        piece(("t3", u), t3, u)
        piece(("t4", u), t4, u)
    b_rows = rows_of((4, "b"))
    piece(("b", 0), got_b, "own", h, *b_rows)
    piece(("b", 1), got_b, "out", h + sgn, *b_rows)
    piece(("b", 2), got_b, "mate", h - sgn, *b_rows)
    piece(("b", 3), got_b, "far1", h + 2, *half_rows(4, lo))
    piece(("b", 4), got_b, "far2", h + 2, *half_rows(4, 1 - lo))

    M = 256
    chunk_rows = 4 * R

    def products(m, g):
        if (m, g) == (0, 0):
            got("cot")
        if m == 0:
            got(("n", g))

        @pl.loop(0, 4)
        def _(yy):
            jj = 4 * g + yy
            rows = pl.ds(m * M, M)
            value = jnp.dot(cot_t[rows, :], nown[jj], preferred_element_type=F32)
            value += jnp.dot(cot_t_in[rows, :], nrecv[jj], preferred_element_type=F32)
            value = value.astype(BF16)
            for k in range(M // chunk_rows):
                for q in range(4):
                    first = k * chunk_rows + q * R
                    part[m * (M // chunk_rows) + k, q, yy, g] = value[first : first + R]

    for m in range(2):
        for g in range(4):
            piece(("p", m, g), products, m, g)

    first_half, second_half = pl.ds(0, 2), pl.ds(2, 2)

    def x_first(k):
        x2, xr, xl = mod(x + 2, 4), mod(x + 1, 4), mod(x - 1, 4)
        send(("xa", 0, k), part.at[k, x2, first_half], xin_a.at[0, k], d_x[1])
        send(("xa", 1, k), part.at[k, x2, second_half], xin_a.at[1, k], d_x[-1])
        send(("xb", 0, k), part.at[k, xr, second_half], xin_b.at[0, k], d_x[1])
        send(("xb", 1, k), part.at[k, xl, first_half], xin_b.at[1, k], d_x[-1])

    def add_into(k, q, half, *others):
        @pl.loop(0, 2)
        def _(i):
            value = part[k, q, half * 2 + i].astype(F32)
            for other in others:
                value += other[i].astype(F32)
            part[k, q, half * 2 + i] = value.astype(BF16)

    def x_relay(way, k):
        q = mod(x + (1, -1)[way], 4)
        got(("xa", way, k))
        add_into(k, q, way, xin_a.at[way, k])
        half = (first_half, second_half)[way]
        send(("xc", way, k), part.at[k, q, half], xin_c.at[way, k], d_x[(1, -1)[way]])

    def x_last(k):
        for way in range(2):
            got(("xb", 1 - way, k))
            got(("xc", way, k))
            add_into(k, x, way, xin_c.at[way, k], xin_b.at[1 - way, k])
        for i, d in enumerate(deltas):
            send(("y", d, k), part.at[k, x, mod(y + d, 4)], yin.at[k, i], d_y[d])

    def y_last(k):
        for d in deltas:
            got(("y", d, k))
        value = part[k, x, y].astype(F32)
        for i in range(3):
            value += yin[k, i].astype(F32)
        z_first(k, value.astype(BF16))

    def z_first(k, value):
        fast = k - (K - FAST)
        if fast >= 0:
            tsf[fast] = value
            zinf[fast, z] = tsf[fast, h]
            for d in range(1, 8):
                send(("z", d, k), tsf.at[fast, mod(z + d, 8) // 2], zinf.at[fast, z], d_z[d])
            return
        ts[k, 0] = value[:, :, :128]
        ts[k, 1] = value[:, :, 128:]
        for d in range(1, 8):
            z_to = mod(z + d, 8)
            send(("z", d, k), ts.at[k, lax.rem(z_to, 2), z_to // 2], zin.at[k, d - 1], d_z[d])

    def y_first(k):
        n = YF.index(k)
        for i, d in enumerate(deltas):
            send(("yf", d, k), part.at[k, pl.ds(0, 4), mod(y + d, 4)], yf_in.at[n, i], d_y[d])

    def y_middle(k):
        n = YF.index(k)
        for d in deltas:
            got(("yf", d, k))

        @pl.loop(0, 4)
        def _(q):
            value = part[k, q, y].astype(F32)
            for i in range(3):
                value += yf_in[n, i, q].astype(F32)
            part[k, q, y] = value.astype(BF16)

        for i, d in enumerate(deltas):
            send(("xd", d, k), part.at[k, mod(x + d, 4), y], xd_in.at[n, i], d_x[d])

    def x_direct_last(k):
        n = YF.index(k)
        for d in deltas:
            got(("xd", d, k))
        value = part[k, x, y].astype(F32)
        for i in range(3):
            value += xd_in[n, i].astype(F32)
        z_first(k, value.astype(BF16))

    def z_last(k):
        for d in range(1, 8):
            got(("z", d, k))
        fast = k - (K - FAST)
        if fast >= 0:
            value = zinf[fast, 0].astype(F32)
            for i in range(1, 8):
                value += zinf[fast, i].astype(F32)
            value = value.astype(BF16)
            wt[k, c, 0, x] = value[:, :128]
            wt[k, c, 1, x] = value[:, 128:]
            ref = wt.at[k, c, pl.ds(0, 2), x]
            send(("gf", 0, k), ref, ref, d_core)
            for d in deltas:
                send(("gf", d, k), ref, ref, d_x[d])
                send(("gg", d, k), ref, ref, d_xf[d])
            return
        value = ts[k, lo, h].astype(F32)
        for d in range(7):
            value += zin[k, d].astype(F32)
        wt[k, c, lo, x] = value.astype(BF16)
        ref = wt.at[k, c, lo, x]
        for d in deltas:
            send(("gx", d, k), ref, ref, d_x[d])

    def node_share(k):
        for d in deltas:
            got(("gx", d, k))
        ref = wt.at[k, c, lo]
        send(("gc", k), ref, ref, d_core)
        send(("gm", k), ref, ref, d_mate)
        send(("gd", k), ref, ref, d_diag)

    def write_block(k):
        if k >= K - FAST:
            got(("gf", 0, k))
            for d in deltas:
                got(("gf", d, k))
                got(("gg", d, k))
        else:
            for n in ("gc", "gm", "gd"):
                got((n, k))
        if (k + 1) * chunk_rows % SEQ == 0:
            first = (k + 1) * chunk_rows // SEQ - 1
            count = SEQ // chunk_rows
            for cc in range(2):
                for ll in range(2):
                    value = wt[pl.ds(first * count, count), cc, ll].astype(F32)
                    value = value.reshape(SEQ, 128)
                    wg_ref[pl.ds(cc * 256 + ll * 128, 128), pl.ds(first * SEQ, SEQ)] = value.T

    for k in range(K):
        if k in YF:
            piece(("yf", k), y_first, k)
            piece(("ym", k), y_middle, k)
            piece(("xd", k), x_direct_last, k)
        else:
            piece(("xf", k), x_first, k)
            piece(("xr", 0, k), x_relay, 0, k)
            piece(("xr", 1, k), x_relay, 1, k)
            piece(("xl", k), x_last, k)
            piece(("yl", k), y_last, k)
        piece(("zl", k), z_last, k)
        if k < K - FAST:
            piece(("ns", k), node_share, k)
        piece(("wr", k), write_block, k)

    acc[...] = jnp.zeros_like(acc)

    def row_grads(group):
        for name in from_core[group]:
            got(name)
        yb = mod(y_of(group), 4)

        @pl.loop(0, 8)
        def _(i):
            block = ((i // 2) * 4 + yb) * 2 + lax.rem(i, 2)
            lanes = pl.ds(pl.multiple_of(block * 256, 256), 256)
            ng = lax.dot_general(
                cot[...], wfull[(i // 2) * 4 + yb, lax.rem(i, 2)], (((1,), (1,)), ((), ())),
                preferred_element_type=F32)
            ngs[block] = ng
            both = ng * tok[:, lanes].astype(F32)
            sums = jnp.sum(both * inverse(), axis=0, keepdims=True)
            gpart[pl.ds(2 * block, 1), :] = sums[:, :128]
            gpart[pl.ds(2 * block + 1, 1), :] = sums[:, 128:]
            both = both * gain_row(block)
            acc[...] += both[:, :128] + both[:, 128:]

    for group in range(4):
        piece(("rg", group), row_grads, group)

    stores = []

    def finish_rows(quarter):
        inv = inverse()
        coef = inv * inv * inv * (jnp.sum(acc[...], axis=1, keepdims=True) / 8192.0)

        @pl.loop(0, 8)
        def _(i):
            block = quarter * 8 + i
            lanes = pl.ds(pl.multiple_of(block * 256, 256), 256)
            value = inv * (gain_row(block) * ngs[block]) - tok[:, lanes].astype(F32) * coef
            tok[:, lanes] = value.astype(BF16)

        lanes = pl.ds(quarter * 2048, 2048)
        copy = pltpu.make_async_copy(tok.at[:, lanes], ig_hbm.at[:, lanes], lsem.at[5 + quarter])
        copy.start()
        stores.append(copy)

    for quarter in range(4):
        piece(("fr", quarter), finish_rows, quarter)

    mine = pl.ds(pl.multiple_of(32 * c, 32), 32)

    def gain_core():
        send("g", gpart, gcore, d_core)

    def gain_x():
        got("g")
        gx[x] = gpart[mine, :] + gcore[mine, :]
        for d in deltas:
            send(("ggx", d), gx.at[x], gx.at[x], d_x[d])

    def gain_y():
        for d in deltas:
            got(("ggx", d))
        gy[y] = (gx[0] + gx[1]) + (gx[2] + gx[3])
        for d in deltas:
            send(("ggy", d), gy.at[y], gy.at[y], d_y[d])

    def gain_z():
        for d in deltas:
            got(("ggy", d))
        gz[z] = (gy[0] + gy[1]) + (gy[2] + gy[3])
        for d in range(1, 8):
            send(("ggz", d), gz.at[z], gz.at[z], d_z[d])

    def gain_last():
        for d in range(1, 8):
            got(("ggz", d))
        total = gz[0]
        for i in range(1, 8):
            total += gz[i]
        gg_ref[mine, :] = total
        send("gg", gg_ref.at[mine], gg_ref.at[mine], d_core)

    for i, fn in enumerate((gain_core, gain_x, gain_y, gain_z, gain_last)):
        piece(("g", i), fn)
    piece(("g", 5), got, "gg")

    for name in ORDER:
        events.pop(name)()
    assert not events and not waits
    for copy in sent:
        copy.wait_send()
    for copy in stores:
        copy.wait()


MESSAGES = 296


def on_device(
    tokens, norm_gain, value_weight, value_grads, new_logprobs, old_logprobs, advantages, lengths
):
    vmem = pl.BlockSpec(memory_space=pltpu.VMEM)
    smem = pl.BlockSpec(memory_space=pltpu.SMEM)
    hbm = pl.BlockSpec(memory_space=pl.ANY)
    input_grads, weight_grads, gain_grads = pl.pallas_call(
        kernel,
        out_shape=(
            jax.ShapeDtypeStruct((256, 8192), BF16),
            jax.ShapeDtypeStruct((512, 512), F32),
            jax.ShapeDtypeStruct((64, 128), F32),
        ),
        in_specs=[hbm, vmem, hbm, vmem, vmem, vmem, smem, smem],
        out_specs=(hbm, vmem, vmem),
        scratch_shapes=[
            pltpu.VMEM((256, 8192), BF16),
            pltpu.VMEM((16, 2, 256, 512), BF16),
            pltpu.VMEM((32, 256, 256), F32),
            pltpu.VMEM((16, 256, 256), BF16),
            pltpu.VMEM((16, 256, 256), BF16),
            pltpu.VMEM((16, 256, 256), BF16),
            pltpu.VMEM((256, 512), BF16),
            pltpu.VMEM((512, 256), BF16),
            pltpu.VMEM((512, 256), BF16),
            pltpu.VMEM((256, 128), F32),
            pltpu.VMEM((256, 128), F32),
            pltpu.VMEM((K, 4, 4, 4, R, 256), BF16),
            pltpu.VMEM((2, K, 2, 4, R, 256), BF16),
            pltpu.VMEM((2, K, 2, 4, R, 256), BF16),
            pltpu.VMEM((2, K, 2, 4, R, 256), BF16),
            pltpu.VMEM((K, 3, 4, R, 256), BF16),
            pltpu.VMEM((K, 2, 4, R, 128), BF16),
            pltpu.VMEM((K, 7, R, 128), BF16),
            pltpu.VMEM((K, 2, 2, 4, R, 128), BF16),
            pltpu.VMEM((max(len(YF), 1), 3, 4, 4, R, 256), BF16),
            pltpu.VMEM((max(len(YF), 1), 3, 4, R, 256), BF16),
            pltpu.VMEM((max(FAST, 1), 4, R, 256), BF16),
            pltpu.VMEM((max(FAST, 1), 8, R, 256), BF16),
            pltpu.VMEM((64, 128), F32),
            pltpu.VMEM((64, 128), F32),
            pltpu.VMEM((4, 32, 128), F32),
            pltpu.VMEM((4, 32, 128), F32),
            pltpu.VMEM((8, 32, 128), F32),
            pltpu.SemaphoreType.DMA((9,)),
            pltpu.SemaphoreType.DMA((MESSAGES,)),
            pltpu.SemaphoreType.DMA((MESSAGES,)),
        ],
        compiler_params=pltpu.CompilerParams(
            collective_id=0, has_side_effects=True, vmem_limit_bytes=54 * 2**20
        ),
    )(
        tokens,
        norm_gain.reshape(64, 128),
        value_weight.reshape(2, 256, 512),
        value_grads,
        new_logprobs.reshape(2, SEQ),
        old_logprobs.reshape(2, SEQ),
        advantages,
        lengths,
    )
    return input_grads, weight_grads, gain_grads.reshape(8192)


def solution(mesh):
    rows = P(("node", "dp"))
    in_specs = (
        P(("node", "dp"), None), P(), P("dp", None), P(("node", "dp"), None), rows, rows, rows, rows,
    )
    out_specs = (P(("node", "dp"), None), P("dp", None), P())
    return jax.shard_map(
        on_device, mesh=mesh, in_specs=in_specs, out_specs=out_specs, check_vma=False
    )
```

```python
import functools

import jax
import jax.numpy as jnp
from jax import lax
from jax.experimental import pallas as pl
from jax.experimental.pallas import tpu as pltpu
from jax.sharding import PartitionSpec as P

SEQ = 128
EPS = 1e-06
K = 8
R = 128 // K
YF = ()
FAST = 4
CUT = 160
ORDER = (
    ("t0", 0, 0), ("t0", 0, 1), ("t0", 4, "b"), ("p", 0, 0), ("p", 0, 1), ("p", 0, 2), ("t0", 1, 0),
    ("t0", 2, 0), ("t1", 0, 0), ("p", 0, 3), ("xf", 0), ("xf", 1), ("p", 1, 0), ("p", 1, 1), ("t1", 0, 1),
    ("p", 1, 2), ("p", 1, 3), ("t0", 3, 0), ("t0", 1, 1), ("t0", 2, 1), ("t1", 4, "b"), ("xr", 0, 0),
    ("t2", 0, 0), ("xr", 1, 0), ("xf", 2), ("t1", 1, 0), ("t0", 3, 1), ("t2", 0, 1), ("xr", 0, 1),
    ("xr", 1, 1), ("xf", 3), ("t1", 2, 0), ("t2", 4, "b"), ("t1", 3, 0), ("b", 0), ("xl", 0), ("t2", 1, 0),
    ("t1", 1, 1), ("xr", 0, 2), ("xr", 1, 2), ("xf", 4), ("t1", 2, 1), ("t2", 2, 0), ("b", 1), ("t2", 3, 0),
    ("t1", 3, 1), ("xl", 1), ("xr", 0, 3), ("xr", 1, 3), ("xf", 5), ("t2", 1, 1), ("t3", 0), ("t3", 4),
    ("t2", 2, 1), ("b", 2), ("xl", 2), ("t2", 3, 1), ("yl", 0), ("xr", 0, 4), ("xr", 1, 4), ("xf", 6),
    ("t3", 1), ("t4", 0), ("yl", 1), ("t4", 4), ("xl", 3), ("t3", 2), ("b", 3), ("rg", 0), ("xr", 0, 5),
    ("xr", 1, 5), ("xf", 7), ("t3", 3), ("yl", 2), ("t4", 1), ("zl", 0), ("xl", 4), ("b", 4), ("zl", 1),
    ("xr", 0, 6), ("xr", 1, 6), ("t4", 2), ("rg", 1), ("t4", 3), ("rg", 2), ("xl", 5), ("zl", 2),
    ("xr", 0, 7), ("xr", 1, 7), ("rg", 3), ("g", 0), ("ns", 0), ("ns", 1), ("yl", 3), ("xl", 6), ("g", 1),
    ("ns", 2), ("yl", 4), ("xl", 7), ("yl", 5), ("wr", 0), ("fr", 0), ("wr", 1), ("fr", 1), ("g", 2),
    ("fr", 2), ("wr", 2), ("yl", 6), ("zl", 3), ("yl", 7), ("zl", 4), ("fr", 3), ("g", 3), ("zl", 5),
    ("ns", 3), ("zl", 6), ("zl", 7), ("g", 4), ("wr", 3), ("wr", 4), ("wr", 5), ("wr", 6), ("g", 5),
    ("wr", 7),
)
MESH = pl.DeviceIdType.MESH
F32 = jnp.float32
BF16 = jnp.bfloat16


def mod(a, n):
    return lax.rem(a + 2 * n, n)


def kernel(
    tok_hbm, gain_ref, w_hbm, vg_ref, new_ref, old_ref, adv_ref, len_ref,
    ig_hbm, wg_ref, gg_ref,
    tok, wfull, ngs, nown, nsend, nrecv, cot, cot_t, cot_t_in, inv_ref, acc,
    part, xin_a, xin_b, xin_c, yin, ts, zin, wt, yf_in, xd_in, tsf, zinf,
    gpart, gcore, gx, gy, gz,
    lsem, ssem, rsem,
):
    node = lax.axis_index("node")
    dp = lax.axis_index("dp")
    c = lax.rem(node, 2)
    x = lax.rem(node // 2, 4)
    lo = node // 8
    h = dp // 4
    y = lax.rem(dp, 4)
    z = 2 * h + lo
    j_me = dp

    def dev(x=x, y=y, z=z, c=c):
        return (lax.rem(z, 2) * 8 + x * 2 + c, (z // 2) * 4 + y)

    sgn = 2 * lo - 1
    z_out = mod(z + sgn, 8)
    z_mate = mod(z - sgn, 8)
    d_core = dev(c=1 - c)
    d_x = {1: dev(x=mod(x + 1, 4)), -1: dev(x=mod(x - 1, 4)), 2: dev(x=mod(x + 2, 4))}
    d_y = {1: dev(y=mod(y + 1, 4)), -1: dev(y=mod(y - 1, 4)), 2: dev(y=mod(y + 2, 4))}
    d_out = dev(z=z_out)
    d_mate = dev(z=z_mate)
    d_z = {d: dev(z=mod(z + d, 8)) for d in range(1, 8)}

    d_diag = dev(z=z_mate, c=1 - c)
    d_xf = {d: dev(x=mod(x + d, 4), c=1 - c) for d in (1, -1, 2)}

    barrier = pltpu.get_barrier_semaphore()
    peers = [d_core, *d_x.values(), *d_xf.values(), *d_y.values(), *d_z.values(), d_diag]
    for peer in peers:
        pl.semaphore_signal(barrier, inc=1, device_id=peer, device_id_type=MESH)

    loads = []
    for r in range(4):
        loads.append(pltpu.make_async_copy(
            tok_hbm.at[pl.ds(r * 64, 64)], tok.at[pl.ds(r * 64, 64)], lsem.at[r]))
    wload = pltpu.make_async_copy(w_hbm, wfull.at[j_me], lsem.at[4])
    for cp in loads:
        cp.start()
    wload.start()

    names = {}
    sent = []

    def message(name, src, dst, device):
        index = names.setdefault(name, len(names))
        return pltpu.make_async_remote_copy(
            src_ref=src, dst_ref=dst, send_sem=ssem.at[index], recv_sem=rsem.at[index],
            device_id=device, device_id_type=MESH)

    waits = {}

    def send(name, src, dst, device):
        copy = message(name, src, dst, device)
        copy.start()
        sent.append(copy)
        waits[name] = copy

    def got(name):
        waits.pop(name).wait_recv()

    row = lax.broadcasted_iota(jnp.int32, (2, SEQ), 0)
    pos = lax.broadcasted_iota(jnp.int32, (2, SEQ), 1)
    adv = jnp.where(row == 0, adv_ref[0], adv_ref[1])
    length = jnp.where(row == 0, len_ref[0], len_ref[1])
    alive = (pos < length).astype(F32)
    ratio = jnp.exp(new_ref[...] - old_ref[...])
    weight = -adv * jnp.clip(ratio, 0.8, 1.2) / SEQ * alive
    eye = lax.broadcasted_iota(jnp.int32, (SEQ, SEQ), 0) == lax.broadcasted_iota(
        jnp.int32, (SEQ, SEQ), 1)
    for s in range(2):
        column = jnp.sum(jnp.where(eye, weight[s : s + 1, :], 0.0), axis=1, keepdims=True)
        wide = column * vg_ref[pl.ds(s * SEQ, SEQ), :].astype(F32)
        cot[pl.ds(s * SEQ, SEQ), :] = wide.astype(BF16)
        cot_t[:, pl.ds(s * SEQ, SEQ)] = wide.T.astype(BF16)

    for r in range(4):
        loads[r].wait()
        rows = pl.ds(r * 64, 64)

        def squares(i, total):
            part_ = tok[rows, pl.ds(pl.multiple_of(i * 512, 512), 512)].astype(F32)
            part_ = part_ * part_
            return total + ((part_[:, :128] + part_[:, 128:256])
                            + (part_[:, 256:384] + part_[:, 384:]))

        total = lax.fori_loop(0, 16, squares, jnp.zeros((64, 128), F32), unroll=2)
        mean = jnp.sum(total, axis=1, keepdims=True) / 8192.0
        inv_ref[rows, :] = jnp.broadcast_to(lax.rsqrt(mean + EPS), (64, 128))

    def inverse():
        return inv_ref[:, 0:1]

    def gain_row(block):
        return jnp.concatenate([gain_ref[pl.ds(2 * block, 1), :], gain_ref[pl.ds(2 * block + 1, 1), :]], axis=1)

    def norm_block(block, dst, jj):
        lanes = pl.ds(pl.multiple_of(block * 256, 256), 256)
        value = tok[:, lanes].astype(F32) * inverse() * gain_row(block)
        dst[jj] = value.astype(BF16)

    @pl.loop(0, 16)
    def _(jj):
        norm_block(2 * jj + (1 - c), nsend, jj)

    @pl.loop(0, 16)
    def _(jj):
        norm_block(2 * jj + c, nown, jj)

    wload.wait()
    pl.semaphore_wait(barrier, len(peers))

    events = {}

    def piece(name, fn, *args):
        events[name] = functools.partial(fn, *args)

    send("cot", cot_t, cot_t_in, d_core)
    for g in range(4):
        send(("n", g), nsend.at[pl.ds(4 * g, 4)], nrecv.at[pl.ds(4 * g, 4)], d_core)

    deltas = (1, -1, 2)

    from_core = {0: [], 1: [], 2: [], 3: []}

    def to_core(name, ref, group):
        send(("k", name), ref, ref, d_core)
        from_core[group].append(("k", name))

    def rows_of(unit):
        if unit[1] == "b":
            return CUT, 256 - CUT
        return unit[1] * (CUT // 2), CUT // 2

    def half_rows(u, which):
        if u == 4:
            return CUT + which * ((256 - CUT) // 2), (256 - CUT) // 2
        return which * (CUT // 2), CUT // 2

    def y_of(u):
        return y + (0, -1, 1, 2, 0)[u]

    def block_rows(hh, yy, base, count):
        return wfull.at[mod(hh, 4) * 4 + mod(yy, 4), c, pl.ds(pl.multiple_of(base, 16), count)]

    def group_of(u):
        return u % 4

    def spread_b(tag, hh, base, count):
        ref = block_rows(hh, y, base, count)
        for d in deltas:
            send(("by", tag, d), ref, ref, d_y[d])

    def got_b(tag, hh, base, count):
        for i, d in enumerate(deltas):
            got(("by", tag, d))
            to_core(("by", tag, d), block_rows(hh, y - d, base, count), i + 1)

    def t0(unit):
        u, s = unit
        base, count = rows_of(unit)
        if u in (1, 2, 3):
            d = deltas[u - 1]
            got(("ay", d, s))
            to_core(("ay", d, s), block_rows(h, y - d, base, count), u)
        ref = block_rows(h, y_of(u), base, count)
        send(("o1", unit), ref, ref, d_out)
        if u == 4:
            spread_b("own", h, base, count)
        elif u == 0:
            for d in deltas:
                send(("ay", d, s), ref, ref, d_y[d])

    def t1(unit):
        u = unit[0]
        base, count = rows_of(unit)
        got(("o1", unit))
        ref = block_rows(h + sgn, y_of(u), base, count)
        send(("m1", unit), ref, ref, d_mate)
        to_core(("o1", unit), ref, group_of(u))
        if u == 4:
            spread_b("out", h + sgn, base, count)

    def t2(unit):
        u, s = unit
        base, count = rows_of(unit)
        got(("m1", unit))
        ref = block_rows(h - sgn, y_of(u), base, count)
        if s != 0:
            half = block_rows(h - sgn, y_of(u), *half_rows(u, 1 - lo))
            send(("o2", u), half, half, d_out)
        to_core(("m1", unit), ref, group_of(u))
        if u == 4:
            spread_b("mate", h - sgn, base, count)

    def t3(u):
        got(("o2", u))
        first, size = half_rows(u, lo)
        ref = block_rows(h + 2, y_of(u), first, size)
        send(("m2", u), ref, ref, d_mate)
        to_core(("o2", u), ref, group_of(u))
        if u == 4:
            spread_b("far1", h + 2, first, size)

    def t4(u):
        got(("m2", u))
        first, size = half_rows(u, 1 - lo)
        ref = block_rows(h + 2, y_of(u), first, size)
        to_core(("m2", u), ref, group_of(u))
        if u == 4:
            spread_b("far2", h + 2, first, size)

    for u in range(5):
        for s in ((0, 1) if u < 4 else ("b",)):
            piece(("t0", u, s), t0, (u, s))
            piece(("t1", u, s), t1, (u, s))
            piece(("t2", u, s), t2, (u, s))
        piece(("t3", u), t3, u)
        piece(("t4", u), t4, u)
    b_rows = rows_of((4, "b"))
    piece(("b", 0), got_b, "own", h, *b_rows)
    piece(("b", 1), got_b, "out", h + sgn, *b_rows)
    piece(("b", 2), got_b, "mate", h - sgn, *b_rows)
    piece(("b", 3), got_b, "far1", h + 2, *half_rows(4, lo))
    piece(("b", 4), got_b, "far2", h + 2, *half_rows(4, 1 - lo))

    M = 256
    chunk_rows = 4 * R

    def products(m, g):
        if (m, g) == (0, 0):
            got("cot")
        if m == 0:
            got(("n", g))

        @pl.loop(0, 4, unroll=4)
        def _(yy):
            jj = 4 * g + yy
            rows = pl.ds(m * M, M)
            value = jnp.dot(cot_t[rows, :], nown[jj], preferred_element_type=F32)
            value += jnp.dot(cot_t_in[rows, :], nrecv[jj], preferred_element_type=F32)
            value = value.astype(BF16)
            for k in range(M // chunk_rows):
                for q in range(4):
                    first = k * chunk_rows + q * R
                    part[m * (M // chunk_rows) + k, q, yy, g] = value[first : first + R]

    for m in range(2):
        for g in range(4):
            piece(("p", m, g), products, m, g)

    first_half, second_half = pl.ds(0, 2), pl.ds(2, 2)

    def x_first(k):
        x2, xr, xl = mod(x + 2, 4), mod(x + 1, 4), mod(x - 1, 4)
        send(("xa", 0, k), part.at[k, x2, first_half], xin_a.at[0, k], d_x[1])
        send(("xa", 1, k), part.at[k, x2, second_half], xin_a.at[1, k], d_x[-1])
        send(("xb", 0, k), part.at[k, xr, second_half], xin_b.at[0, k], d_x[1])
        send(("xb", 1, k), part.at[k, xl, first_half], xin_b.at[1, k], d_x[-1])

    def add_into(k, q, half, *others):
        @pl.loop(0, 2, unroll=2)
        def _(i):
            value = part[k, q, half * 2 + i].astype(F32)
            for other in others:
                value += other[i].astype(F32)
            part[k, q, half * 2 + i] = value.astype(BF16)

    def x_relay(way, k):
        q = mod(x + (1, -1)[way], 4)
        got(("xa", way, k))
        add_into(k, q, way, xin_a.at[way, k])
        half = (first_half, second_half)[way]
        send(("xc", way, k), part.at[k, q, half], xin_c.at[way, k], d_x[(1, -1)[way]])

    def x_last(k):
        for way in range(2):
            got(("xb", 1 - way, k))
            got(("xc", way, k))
            add_into(k, x, way, xin_c.at[way, k], xin_b.at[1 - way, k])
        for i, d in enumerate(deltas):
            send(("y", d, k), part.at[k, x, mod(y + d, 4)], yin.at[k, i], d_y[d])

    def y_last(k):
        for d in deltas:
            got(("y", d, k))
        value = part[k, x, y].astype(F32)
        for i in range(3):
            value += yin[k, i].astype(F32)
        z_first(k, value.astype(BF16))

    def z_first(k, value):
        fast = k - (K - FAST)
        if fast >= 0:
            tsf[fast] = value
            zinf[fast, z] = tsf[fast, h]
            for d in range(1, 8):
                send(("z", d, k), tsf.at[fast, mod(z + d, 8) // 2], zinf.at[fast, z], d_z[d])
            return
        ts[k, 0] = value[:, :, :128]
        ts[k, 1] = value[:, :, 128:]
        for d in range(1, 8):
            z_to = mod(z + d, 8)
            send(("z", d, k), ts.at[k, lax.rem(z_to, 2), z_to // 2], zin.at[k, d - 1], d_z[d])

    def y_first(k):
        n = YF.index(k)
        for i, d in enumerate(deltas):
            send(("yf", d, k), part.at[k, pl.ds(0, 4), mod(y + d, 4)], yf_in.at[n, i], d_y[d])

    def y_middle(k):
        n = YF.index(k)
        for d in deltas:
            got(("yf", d, k))

        @pl.loop(0, 4)
        def _(q):
            value = part[k, q, y].astype(F32)
            for i in range(3):
                value += yf_in[n, i, q].astype(F32)
            part[k, q, y] = value.astype(BF16)

        for i, d in enumerate(deltas):
            send(("xd", d, k), part.at[k, mod(x + d, 4), y], xd_in.at[n, i], d_x[d])

    def x_direct_last(k):
        n = YF.index(k)
        for d in deltas:
            got(("xd", d, k))
        value = part[k, x, y].astype(F32)
        for i in range(3):
            value += xd_in[n, i].astype(F32)
        z_first(k, value.astype(BF16))

    def z_last(k):
        for d in range(1, 8):
            got(("z", d, k))
        fast = k - (K - FAST)
        if fast >= 0:
            value = zinf[fast, 0].astype(F32)
            for i in range(1, 8):
                value += zinf[fast, i].astype(F32)
            value = value.astype(BF16)
            wt[k, c, 0, x] = value[:, :128]
            wt[k, c, 1, x] = value[:, 128:]
            ref = wt.at[k, c, pl.ds(0, 2), x]
            send(("gf", 0, k), ref, ref, d_core)
            for d in deltas:
                send(("gf", d, k), ref, ref, d_x[d])
                send(("gg", d, k), ref, ref, d_xf[d])
            return
        value = ts[k, lo, h].astype(F32)
        for d in range(7):
            value += zin[k, d].astype(F32)
        wt[k, c, lo, x] = value.astype(BF16)
        ref = wt.at[k, c, lo, x]
        for d in deltas:
            send(("gx", d, k), ref, ref, d_x[d])

    def node_share(k):
        for d in deltas:
            got(("gx", d, k))
        ref = wt.at[k, c, lo]
        send(("gc", k), ref, ref, d_core)
        send(("gm", k), ref, ref, d_mate)
        send(("gd", k), ref, ref, d_diag)

    def write_block(k):
        if k >= K - FAST:
            got(("gf", 0, k))
            for d in deltas:
                got(("gf", d, k))
                got(("gg", d, k))
        else:
            for n in ("gc", "gm", "gd"):
                got((n, k))
        if (k + 1) * chunk_rows % SEQ == 0:
            first = (k + 1) * chunk_rows // SEQ - 1
            count = SEQ // chunk_rows
            for cc in range(2):
                for ll in range(2):
                    value = wt[pl.ds(first * count, count), cc, ll].astype(F32)
                    value = value.reshape(SEQ, 128)
                    wg_ref[pl.ds(cc * 256 + ll * 128, 128), pl.ds(first * SEQ, SEQ)] = value.T

    for k in range(K):
        if k in YF:
            piece(("yf", k), y_first, k)
            piece(("ym", k), y_middle, k)
            piece(("xd", k), x_direct_last, k)
        else:
            piece(("xf", k), x_first, k)
            piece(("xr", 0, k), x_relay, 0, k)
            piece(("xr", 1, k), x_relay, 1, k)
            piece(("xl", k), x_last, k)
            piece(("yl", k), y_last, k)
        piece(("zl", k), z_last, k)
        if k < K - FAST:
            piece(("ns", k), node_share, k)
        piece(("wr", k), write_block, k)

    acc[...] = jnp.zeros_like(acc)

    def row_grads(group):
        for name in from_core[group]:
            got(name)
        yb = mod(y_of(group), 4)

        @pl.loop(0, 8, unroll=4)
        def _(i):
            block = ((i // 2) * 4 + yb) * 2 + lax.rem(i, 2)
            lanes = pl.ds(pl.multiple_of(block * 256, 256), 256)
            ng = lax.dot_general(
                cot[...], wfull[(i // 2) * 4 + yb, lax.rem(i, 2)], (((1,), (1,)), ((), ())),
                preferred_element_type=F32)
            ngs[block] = ng
            both = ng * tok[:, lanes].astype(F32)
            sums = jnp.sum(both * inverse(), axis=0, keepdims=True)
            gpart[pl.ds(2 * block, 1), :] = sums[:, :128]
            gpart[pl.ds(2 * block + 1, 1), :] = sums[:, 128:]
            both = both * gain_row(block)
            acc[...] += both[:, :128] + both[:, 128:]

    for group in range(4):
        piece(("rg", group), row_grads, group)

    stores = []

    def finish_rows(quarter):
        inv = inverse()
        coef = inv * inv * inv * (jnp.sum(acc[...], axis=1, keepdims=True) / 8192.0)

        @pl.loop(0, 8, unroll=2)
        def _(i):
            block = quarter * 8 + i
            lanes = pl.ds(pl.multiple_of(block * 256, 256), 256)
            value = inv * (gain_row(block) * ngs[block]) - tok[:, lanes].astype(F32) * coef
            tok[:, lanes] = value.astype(BF16)

        lanes = pl.ds(quarter * 2048, 2048)
        copy = pltpu.make_async_copy(tok.at[:, lanes], ig_hbm.at[:, lanes], lsem.at[5 + quarter])
        copy.start()
        stores.append(copy)

    for quarter in range(4):
        piece(("fr", quarter), finish_rows, quarter)

    mine = pl.ds(pl.multiple_of(32 * c, 32), 32)

    def gain_core():
        send("g", gpart, gcore, d_core)

    def gain_x():
        got("g")
        gx[x] = gpart[mine, :] + gcore[mine, :]
        for d in deltas:
            send(("ggx", d), gx.at[x], gx.at[x], d_x[d])

    def gain_y():
        for d in deltas:
            got(("ggx", d))
        gy[y] = (gx[0] + gx[1]) + (gx[2] + gx[3])
        for d in deltas:
            send(("ggy", d), gy.at[y], gy.at[y], d_y[d])

    def gain_z():
        for d in deltas:
            got(("ggy", d))
        gz[z] = (gy[0] + gy[1]) + (gy[2] + gy[3])
        for d in range(1, 8):
            send(("ggz", d), gz.at[z], gz.at[z], d_z[d])

    def gain_last():
        for d in range(1, 8):
            got(("ggz", d))
        total = gz[0]
        for i in range(1, 8):
            total += gz[i]
        gg_ref[mine, :] = total
        send("gg", gg_ref.at[mine], gg_ref.at[mine], d_core)

    for i, fn in enumerate((gain_core, gain_x, gain_y, gain_z, gain_last)):
        piece(("g", i), fn)
    piece(("g", 5), got, "gg")

    for name in ORDER:
        events.pop(name)()
    assert not events and not waits
    for copy in sent:
        copy.wait_send()
    for copy in stores:
        copy.wait()


MESSAGES = 298


def on_device(
    tokens, norm_gain, value_weight, value_grads, new_logprobs, old_logprobs, advantages, lengths
):
    vmem = pl.BlockSpec(memory_space=pltpu.VMEM)
    smem = pl.BlockSpec(memory_space=pltpu.SMEM)
    hbm = pl.BlockSpec(memory_space=pl.ANY)
    input_grads, weight_grads, gain_grads = pl.pallas_call(
        kernel,
        out_shape=(
            jax.ShapeDtypeStruct((256, 8192), BF16),
            jax.ShapeDtypeStruct((512, 512), F32),
            jax.ShapeDtypeStruct((64, 128), F32),
        ),
        in_specs=[hbm, vmem, hbm, vmem, vmem, vmem, smem, smem],
        out_specs=(hbm, vmem, vmem),
        scratch_shapes=[
            pltpu.VMEM((256, 8192), BF16),
            pltpu.VMEM((16, 2, 256, 512), BF16),
            pltpu.VMEM((32, 256, 256), F32),
            pltpu.VMEM((16, 256, 256), BF16),
            pltpu.VMEM((16, 256, 256), BF16),
            pltpu.VMEM((16, 256, 256), BF16),
            pltpu.VMEM((256, 512), BF16),
            pltpu.VMEM((512, 256), BF16),
            pltpu.VMEM((512, 256), BF16),
            pltpu.VMEM((256, 128), F32),
            pltpu.VMEM((256, 128), F32),
            pltpu.VMEM((K, 4, 4, 4, R, 256), BF16),
            pltpu.VMEM((2, K, 2, 4, R, 256), BF16),
            pltpu.VMEM((2, K, 2, 4, R, 256), BF16),
            pltpu.VMEM((2, K, 2, 4, R, 256), BF16),
            pltpu.VMEM((K, 3, 4, R, 256), BF16),
            pltpu.VMEM((K, 2, 4, R, 128), BF16),
            pltpu.VMEM((K, 7, R, 128), BF16),
            pltpu.VMEM((K, 2, 2, 4, R, 128), BF16),
            pltpu.VMEM((max(len(YF), 1), 3, 4, 4, R, 256), BF16),
            pltpu.VMEM((max(len(YF), 1), 3, 4, R, 256), BF16),
            pltpu.VMEM((max(FAST, 1), 4, R, 256), BF16),
            pltpu.VMEM((max(FAST, 1), 8, R, 256), BF16),
            pltpu.VMEM((64, 128), F32),
            pltpu.VMEM((64, 128), F32),
            pltpu.VMEM((4, 32, 128), F32),
            pltpu.VMEM((4, 32, 128), F32),
            pltpu.VMEM((8, 32, 128), F32),
            pltpu.SemaphoreType.DMA((9,)),
            pltpu.SemaphoreType.DMA((MESSAGES,)),
            pltpu.SemaphoreType.DMA((MESSAGES,)),
        ],
        compiler_params=pltpu.CompilerParams(
            collective_id=0, has_side_effects=True, vmem_limit_bytes=54 * 2**20
        ),
    )(
        tokens,
        norm_gain.reshape(64, 128),
        value_weight.reshape(2, 256, 512),
        value_grads,
        new_logprobs.reshape(2, SEQ),
        old_logprobs.reshape(2, SEQ),
        advantages,
        lengths,
    )
    return input_grads, weight_grads, gain_grads.reshape(8192)


def solution(mesh):
    rows = P(("node", "dp"))
    in_specs = (
        P(("node", "dp"), None), P(), P("dp", None), P(("node", "dp"), None), rows, rows, rows, rows,
    )
    out_specs = (P(("node", "dp"), None), P("dp", None), P())
    return jax.shard_map(
        on_device, mesh=mesh, in_specs=in_specs, out_specs=out_specs, check_vma=False
    )
```

```python
import functools

import jax
import jax.numpy as jnp
from jax import lax
from jax.experimental import pallas as pl
from jax.experimental.pallas import tpu as pltpu
from jax.sharding import PartitionSpec as P

SEQ = 128
EPS = 1e-06
K = 8
R = 128 // K
YF = ()
FAST = 4
CUT = 160
ORDER = (
    ("t0", 0, 0), ("t0", 0, 1), ("t0", 4, "b"), ("p", 0, 0), ("xg", 0), ("p", 0, 1), ("xg", 1), ("p", 0, 2),
    ("xg", 2), ("t0", 1, 0), ("p", 0, 3), ("xg", 3), ("t1", 0, 0), ("xf", 1), ("xf", 2), ("xf", 3),
    ("t0", 2, 0), ("p", 1, 0), ("t1", 0, 1), ("p", 1, 1), ("t0", 3, 0), ("p", 1, 2), ("p", 1, 3),
    ("xr", 0, 0), ("xr", 1, 0), ("t1", 4, "b"), ("t0", 1, 1), ("t0", 2, 1), ("xr", 0, 1), ("xr", 1, 1),
    ("t2", 0, 0), ("t1", 1, 0), ("xf", 4), ("t0", 3, 1), ("t2", 0, 1), ("t1", 2, 0), ("xr", 0, 2),
    ("xr", 1, 2), ("xf", 5), ("t2", 4, "b"), ("t1", 3, 0), ("b", 0), ("xr", 0, 3), ("xr", 1, 3), ("t2", 1, 0),
    ("t1", 1, 1), ("xf", 6), ("t2", 2, 0), ("t1", 2, 1), ("xl", 0), ("t2", 3, 0), ("b", 1), ("t1", 3, 1),
    ("xl", 1), ("t2", 1, 1), ("t3", 0), ("xr", 0, 4), ("xr", 1, 4), ("xf", 7), ("t3", 4), ("t2", 2, 1),
    ("b", 2), ("xl", 2), ("t2", 3, 1), ("yl", 0), ("xr", 0, 5), ("xr", 1, 5), ("t4", 0), ("t3", 1), ("yl", 1),
    ("t4", 4), ("t3", 2), ("rg", 0), ("t3", 3), ("b", 3), ("xl", 3), ("xr", 0, 6), ("xr", 1, 6), ("t4", 1),
    ("yl", 2), ("zl", 0), ("b", 4), ("xl", 4), ("zl", 1), ("t4", 2), ("xr", 0, 7), ("xr", 1, 7), ("rg", 1),
    ("t4", 3), ("rg", 2), ("xl", 5), ("rg", 3), ("g", 0), ("xl", 6), ("ns", 0), ("ns", 1), ("g", 1),
    ("yl", 3), ("xl", 7), ("yl", 4), ("fr", 0), ("yl", 5), ("wr", 0), ("fr", 1), ("g", 2), ("wr", 1),
    ("yl", 6), ("fr", 2), ("fr", 3), ("yl", 7), ("zl", 2), ("zl", 3), ("g", 3), ("zl", 4), ("zl", 5),
    ("zl", 6), ("ns", 2), ("ns", 3), ("zl", 7), ("g", 4), ("wr", 2), ("g", 5), ("wr", 3), ("wr", 4),
    ("wr", 5), ("wr", 6), ("wr", 7),
)
MESH = pl.DeviceIdType.MESH
F32 = jnp.float32
BF16 = jnp.bfloat16


def mod(a, n):
    return lax.rem(a + 2 * n, n)


def kernel(
    tok_hbm, gain_ref, w_hbm, vg_ref, new_ref, old_ref, adv_ref, len_ref,
    ig_hbm, wg_ref, gg_ref,
    tok, wfull, ngs, nown, nsend, nrecv, cot, cot_t, cot_t_in, inv_ref, acc,
    part, xin_a, xin_b, xin_c, yin, ts, zin, wt, yf_in, xd_in, tsf, zinf,
    gpart, gcore, gx, gy, gz,
    lsem, ssem, rsem,
):
    node = lax.axis_index("node")
    dp = lax.axis_index("dp")
    c = lax.rem(node, 2)
    x = lax.rem(node // 2, 4)
    lo = node // 8
    h = dp // 4
    y = lax.rem(dp, 4)
    z = 2 * h + lo
    j_me = dp

    def dev(x=x, y=y, z=z, c=c):
        return (lax.rem(z, 2) * 8 + x * 2 + c, (z // 2) * 4 + y)

    sgn = 2 * lo - 1
    z_out = mod(z + sgn, 8)
    z_mate = mod(z - sgn, 8)
    d_core = dev(c=1 - c)
    d_x = {1: dev(x=mod(x + 1, 4)), -1: dev(x=mod(x - 1, 4)), 2: dev(x=mod(x + 2, 4))}
    d_y = {1: dev(y=mod(y + 1, 4)), -1: dev(y=mod(y - 1, 4)), 2: dev(y=mod(y + 2, 4))}
    d_out = dev(z=z_out)
    d_mate = dev(z=z_mate)
    d_z = {d: dev(z=mod(z + d, 8)) for d in range(1, 8)}

    d_diag = dev(z=z_mate, c=1 - c)
    d_xf = {d: dev(x=mod(x + d, 4), c=1 - c) for d in (1, -1, 2)}

    barrier = pltpu.get_barrier_semaphore()
    peers = [d_core, *d_x.values(), *d_xf.values(), *d_y.values(), *d_z.values(), d_diag]
    for peer in peers:
        pl.semaphore_signal(barrier, inc=1, device_id=peer, device_id_type=MESH)

    loads = []
    for r in range(4):
        loads.append(pltpu.make_async_copy(
            tok_hbm.at[pl.ds(r * 64, 64)], tok.at[pl.ds(r * 64, 64)], lsem.at[r]))
    wload = pltpu.make_async_copy(w_hbm, wfull.at[j_me], lsem.at[4])
    for cp in loads:
        cp.start()
    wload.start()

    names = {}
    sent = []

    def message(name, src, dst, device):
        index = names.setdefault(name, len(names))
        return pltpu.make_async_remote_copy(
            src_ref=src, dst_ref=dst, send_sem=ssem.at[index], recv_sem=rsem.at[index],
            device_id=device, device_id_type=MESH)

    waits = {}

    def send(name, src, dst, device):
        copy = message(name, src, dst, device)
        copy.start()
        sent.append(copy)
        waits[name] = copy

    def got(name):
        waits.pop(name).wait_recv()

    row = lax.broadcasted_iota(jnp.int32, (2, SEQ), 0)
    pos = lax.broadcasted_iota(jnp.int32, (2, SEQ), 1)
    adv = jnp.where(row == 0, adv_ref[0], adv_ref[1])
    length = jnp.where(row == 0, len_ref[0], len_ref[1])
    alive = (pos < length).astype(F32)
    ratio = jnp.exp(new_ref[...] - old_ref[...])
    weight = -adv * jnp.clip(ratio, 0.8, 1.2) / SEQ * alive
    eye = lax.broadcasted_iota(jnp.int32, (SEQ, SEQ), 0) == lax.broadcasted_iota(
        jnp.int32, (SEQ, SEQ), 1)
    for s in range(2):
        column = jnp.sum(jnp.where(eye, weight[s : s + 1, :], 0.0), axis=1, keepdims=True)
        wide = column * vg_ref[pl.ds(s * SEQ, SEQ), :].astype(F32)
        cot[pl.ds(s * SEQ, SEQ), :] = wide.astype(BF16)
        cot_t[:, pl.ds(s * SEQ, SEQ)] = wide.T.astype(BF16)

    for r in range(4):
        loads[r].wait()
        rows = pl.ds(r * 64, 64)

        def squares(i, total):
            part_ = tok[rows, pl.ds(pl.multiple_of(i * 512, 512), 512)].astype(F32)
            part_ = part_ * part_
            return total + ((part_[:, :128] + part_[:, 128:256])
                            + (part_[:, 256:384] + part_[:, 384:]))

        total = lax.fori_loop(0, 16, squares, jnp.zeros((64, 128), F32), unroll=2)
        mean = jnp.sum(total, axis=1, keepdims=True) / 8192.0
        inv_ref[rows, :] = jnp.broadcast_to(lax.rsqrt(mean + EPS), (64, 128))

    def inverse():
        return inv_ref[:, 0:1]

    def gain_row(block):
        return jnp.concatenate([gain_ref[pl.ds(2 * block, 1), :], gain_ref[pl.ds(2 * block + 1, 1), :]], axis=1)

    def norm_block(block, dst, jj):
        lanes = pl.ds(pl.multiple_of(block * 256, 256), 256)
        value = tok[:, lanes].astype(F32) * inverse() * gain_row(block)
        dst[jj] = value.astype(BF16)

    @pl.loop(0, 16)
    def _(jj):
        norm_block(2 * jj + (1 - c), nsend, jj)

    @pl.loop(0, 16)
    def _(jj):
        norm_block(2 * jj + c, nown, jj)

    wload.wait()
    pl.semaphore_wait(barrier, len(peers))

    events = {}

    def piece(name, fn, *args):
        events[name] = functools.partial(fn, *args)

    send("cot", cot_t, cot_t_in, d_core)
    for g in range(4):
        send(("n", g), nsend.at[pl.ds(4 * g, 4)], nrecv.at[pl.ds(4 * g, 4)], d_core)

    deltas = (1, -1, 2)

    from_core = {0: [], 1: [], 2: [], 3: []}

    def to_core(name, ref, group):
        send(("k", name), ref, ref, d_core)
        from_core[group].append(("k", name))

    def rows_of(unit):
        if unit[1] == "b":
            return CUT, 256 - CUT
        return unit[1] * (CUT // 2), CUT // 2

    def half_rows(u, which):
        if u == 4:
            return CUT + which * ((256 - CUT) // 2), (256 - CUT) // 2
        return which * (CUT // 2), CUT // 2

    def y_of(u):
        return y + (0, -1, 1, 2, 0)[u]

    def block_rows(hh, yy, base, count):
        return wfull.at[mod(hh, 4) * 4 + mod(yy, 4), c, pl.ds(pl.multiple_of(base, 16), count)]

    def group_of(u):
        return u % 4

    def spread_b(tag, hh, base, count):
        ref = block_rows(hh, y, base, count)
        for d in deltas:
            send(("by", tag, d), ref, ref, d_y[d])

    def got_b(tag, hh, base, count):
        for i, d in enumerate(deltas):
            got(("by", tag, d))
            to_core(("by", tag, d), block_rows(hh, y - d, base, count), i + 1)

    def t0(unit):
        u, s = unit
        base, count = rows_of(unit)
        if u in (1, 2, 3):
            d = deltas[u - 1]
            got(("ay", d, s))
            to_core(("ay", d, s), block_rows(h, y - d, base, count), u)
        ref = block_rows(h, y_of(u), base, count)
        send(("o1", unit), ref, ref, d_out)
        if u == 4:
            spread_b("own", h, base, count)
        elif u == 0:
            for d in deltas:
                send(("ay", d, s), ref, ref, d_y[d])

    def t1(unit):
        u = unit[0]
        base, count = rows_of(unit)
        got(("o1", unit))
        ref = block_rows(h + sgn, y_of(u), base, count)
        send(("m1", unit), ref, ref, d_mate)
        to_core(("o1", unit), ref, group_of(u))
        if u == 4:
            spread_b("out", h + sgn, base, count)

    def t2(unit):
        u, s = unit
        base, count = rows_of(unit)
        got(("m1", unit))
        ref = block_rows(h - sgn, y_of(u), base, count)
        if s != 0:
            half = block_rows(h - sgn, y_of(u), *half_rows(u, 1 - lo))
            send(("o2", u), half, half, d_out)
        to_core(("m1", unit), ref, group_of(u))
        if u == 4:
            spread_b("mate", h - sgn, base, count)

    def t3(u):
        got(("o2", u))
        first, size = half_rows(u, lo)
        ref = block_rows(h + 2, y_of(u), first, size)
        send(("m2", u), ref, ref, d_mate)
        to_core(("o2", u), ref, group_of(u))
        if u == 4:
            spread_b("far1", h + 2, first, size)

    def t4(u):
        got(("m2", u))
        first, size = half_rows(u, 1 - lo)
        ref = block_rows(h + 2, y_of(u), first, size)
        to_core(("m2", u), ref, group_of(u))
        if u == 4:
            spread_b("far2", h + 2, first, size)

    for u in range(5):
        for s in ((0, 1) if u < 4 else ("b",)):
            piece(("t0", u, s), t0, (u, s))
            piece(("t1", u, s), t1, (u, s))
            piece(("t2", u, s), t2, (u, s))
        piece(("t3", u), t3, u)
        piece(("t4", u), t4, u)
    b_rows = rows_of((4, "b"))
    piece(("b", 0), got_b, "own", h, *b_rows)
    piece(("b", 1), got_b, "out", h + sgn, *b_rows)
    piece(("b", 2), got_b, "mate", h - sgn, *b_rows)
    piece(("b", 3), got_b, "far1", h + 2, *half_rows(4, lo))
    piece(("b", 4), got_b, "far2", h + 2, *half_rows(4, 1 - lo))

    M = 256
    chunk_rows = 4 * R

    def products(m, g):
        if (m, g) == (0, 0):
            got("cot")
        if m == 0:
            got(("n", g))

        @pl.loop(0, 4, unroll=4)
        def _(yy):
            jj = 4 * g + yy
            rows = pl.ds(m * M, M)
            value = jnp.dot(cot_t[rows, :], nown[jj], preferred_element_type=F32)
            value += jnp.dot(cot_t_in[rows, :], nrecv[jj], preferred_element_type=F32)
            value = value.astype(BF16)
            for k in range(M // chunk_rows):
                for q in range(4):
                    first = k * chunk_rows + q * R
                    part[m * (M // chunk_rows) + k, q, yy, g] = value[first : first + R]

    for m in range(2):
        for g in range(4):
            piece(("p", m, g), products, m, g)

    first_half, second_half = pl.ds(0, 2), pl.ds(2, 2)

    def x_first(k):
        x2, xr, xl = mod(x + 2, 4), mod(x + 1, 4), mod(x - 1, 4)
        send(("xa", 0, k), part.at[k, x2, first_half], xin_a.at[0, k], d_x[1])
        send(("xa", 1, k), part.at[k, x2, second_half], xin_a.at[1, k], d_x[-1])
        send(("xb", 0, k), part.at[k, xr, second_half], xin_b.at[0, k], d_x[1])
        send(("xb", 1, k), part.at[k, xl, first_half], xin_b.at[1, k], d_x[-1])

    def x_early(g):
        x2, xr, xl = mod(x + 2, 4), mod(x + 1, 4), mod(x - 1, 4)
        for kind, way, q, half, into in (
            ("xa", 0, x2, first_half, xin_a), ("xa", 1, x2, second_half, xin_a),
            ("xb", 0, xr, second_half, xin_b), ("xb", 1, xl, first_half, xin_b),
        ):
            send((kind, way, 0, g), part.at[0, q, half, g], into.at[way, 0, pl.ds(0, 2), g],
                 d_x[(1, -1)[way]])

    def got_x(kind, way, k):
        if k == 0:
            for g in range(4):
                got((kind, way, 0, g))
        else:
            got((kind, way, k))

    def add_into(k, q, half, *others):
        @pl.loop(0, 2, unroll=2)
        def _(i):
            value = part[k, q, half * 2 + i].astype(F32)
            for other in others:
                value += other[i].astype(F32)
            part[k, q, half * 2 + i] = value.astype(BF16)

    def x_relay(way, k):
        q = mod(x + (1, -1)[way], 4)
        got_x("xa", way, k)
        add_into(k, q, way, xin_a.at[way, k])
        half = (first_half, second_half)[way]
        send(("xc", way, k), part.at[k, q, half], xin_c.at[way, k], d_x[(1, -1)[way]])

    def x_last(k):
        for way in range(2):
            got_x("xb", 1 - way, k)
            got(("xc", way, k))
            add_into(k, x, way, xin_c.at[way, k], xin_b.at[1 - way, k])
        for i, d in enumerate(deltas):
            send(("y", d, k), part.at[k, x, mod(y + d, 4)], yin.at[k, i], d_y[d])

    def y_last(k):
        for d in deltas:
            got(("y", d, k))
        value = part[k, x, y].astype(F32)
        for i in range(3):
            value += yin[k, i].astype(F32)
        z_first(k, value.astype(BF16))

    def z_first(k, value):
        fast = k - (K - FAST)
        if fast >= 0:
            tsf[fast] = value
            zinf[fast, z] = tsf[fast, h]
            for d in range(1, 8):
                send(("z", d, k), tsf.at[fast, mod(z + d, 8) // 2], zinf.at[fast, z], d_z[d])
            return
        ts[k, 0] = value[:, :, :128]
        ts[k, 1] = value[:, :, 128:]
        for d in range(1, 8):
            z_to = mod(z + d, 8)
            send(("z", d, k), ts.at[k, lax.rem(z_to, 2), z_to // 2], zin.at[k, d - 1], d_z[d])

    def y_first(k):
        n = YF.index(k)
        for i, d in enumerate(deltas):
            send(("yf", d, k), part.at[k, pl.ds(0, 4), mod(y + d, 4)], yf_in.at[n, i], d_y[d])

    def y_middle(k):
        n = YF.index(k)
        for d in deltas:
            got(("yf", d, k))

        @pl.loop(0, 4)
        def _(q):
            value = part[k, q, y].astype(F32)
            for i in range(3):
                value += yf_in[n, i, q].astype(F32)
            part[k, q, y] = value.astype(BF16)

        for i, d in enumerate(deltas):
            send(("xd", d, k), part.at[k, mod(x + d, 4), y], xd_in.at[n, i], d_x[d])

    def x_direct_last(k):
        n = YF.index(k)
        for d in deltas:
            got(("xd", d, k))
        value = part[k, x, y].astype(F32)
        for i in range(3):
            value += xd_in[n, i].astype(F32)
        z_first(k, value.astype(BF16))

    def z_last(k):
        for d in range(1, 8):
            got(("z", d, k))
        fast = k - (K - FAST)
        if fast >= 0:
            value = zinf[fast, 0].astype(F32)
            for i in range(1, 8):
                value += zinf[fast, i].astype(F32)
            value = value.astype(BF16)
            wt[k, c, 0, x] = value[:, :128]
            wt[k, c, 1, x] = value[:, 128:]
            ref = wt.at[k, c, pl.ds(0, 2), x]
            send(("gf", 0, k), ref, ref, d_core)
            for d in deltas:
                send(("gf", d, k), ref, ref, d_x[d])
                send(("gg", d, k), ref, ref, d_xf[d])
            return
        value = ts[k, lo, h].astype(F32)
        for d in range(7):
            value += zin[k, d].astype(F32)
        wt[k, c, lo, x] = value.astype(BF16)
        ref = wt.at[k, c, lo, x]
        for d in deltas:
            send(("gx", d, k), ref, ref, d_x[d])

    def node_share(k):
        for d in deltas:
            got(("gx", d, k))
        ref = wt.at[k, c, lo]
        send(("gc", k), ref, ref, d_core)
        send(("gm", k), ref, ref, d_mate)
        send(("gd", k), ref, ref, d_diag)

    def write_block(k):
        if k >= K - FAST:
            got(("gf", 0, k))
            for d in deltas:
                got(("gf", d, k))
                got(("gg", d, k))
        else:
            for n in ("gc", "gm", "gd"):
                got((n, k))
        if (k + 1) * chunk_rows % SEQ == 0:
            first = (k + 1) * chunk_rows // SEQ - 1
            count = SEQ // chunk_rows
            for cc in range(2):
                for ll in range(2):
                    value = wt[pl.ds(first * count, count), cc, ll].astype(F32)
                    value = value.reshape(SEQ, 128)
                    wg_ref[pl.ds(cc * 256 + ll * 128, 128), pl.ds(first * SEQ, SEQ)] = value.T

    for k in range(K):
        if k in YF:
            piece(("yf", k), y_first, k)
            piece(("ym", k), y_middle, k)
            piece(("xd", k), x_direct_last, k)
        else:
            if k == 0:
                for g in range(4):
                    piece(("xg", g), x_early, g)
            else:
                piece(("xf", k), x_first, k)
            piece(("xr", 0, k), x_relay, 0, k)
            piece(("xr", 1, k), x_relay, 1, k)
            piece(("xl", k), x_last, k)
            piece(("yl", k), y_last, k)
        piece(("zl", k), z_last, k)
        if k < K - FAST:
            piece(("ns", k), node_share, k)
        piece(("wr", k), write_block, k)

    acc[...] = jnp.zeros_like(acc)

    def row_grads(group):
        for name in from_core[group]:
            got(name)
        yb = mod(y_of(group), 4)

        @pl.loop(0, 8, unroll=4)
        def _(i):
            block = ((i // 2) * 4 + yb) * 2 + lax.rem(i, 2)
            lanes = pl.ds(pl.multiple_of(block * 256, 256), 256)
            ng = lax.dot_general(
                cot[...], wfull[(i // 2) * 4 + yb, lax.rem(i, 2)], (((1,), (1,)), ((), ())),
                preferred_element_type=F32)
            ngs[block] = ng
            both = ng * tok[:, lanes].astype(F32)
            sums = jnp.sum(both * inverse(), axis=0, keepdims=True)
            gpart[pl.ds(2 * block, 1), :] = sums[:, :128]
            gpart[pl.ds(2 * block + 1, 1), :] = sums[:, 128:]
            both = both * gain_row(block)
            acc[...] += both[:, :128] + both[:, 128:]

    for group in range(4):
        piece(("rg", group), row_grads, group)

    stores = []

    def finish_rows(quarter):
        inv = inverse()
        coef = inv * inv * inv * (jnp.sum(acc[...], axis=1, keepdims=True) / 8192.0)

        @pl.loop(0, 8, unroll=2)
        def _(i):
            block = quarter * 8 + i
            lanes = pl.ds(pl.multiple_of(block * 256, 256), 256)
            value = inv * (gain_row(block) * ngs[block]) - tok[:, lanes].astype(F32) * coef
            tok[:, lanes] = value.astype(BF16)

        lanes = pl.ds(quarter * 2048, 2048)
        copy = pltpu.make_async_copy(tok.at[:, lanes], ig_hbm.at[:, lanes], lsem.at[5 + quarter])
        copy.start()
        stores.append(copy)

    for quarter in range(4):
        piece(("fr", quarter), finish_rows, quarter)

    mine = pl.ds(pl.multiple_of(32 * c, 32), 32)

    def gain_core():
        send("g", gpart, gcore, d_core)

    def gain_x():
        got("g")
        gx[x] = gpart[mine, :] + gcore[mine, :]
        for d in deltas:
            send(("ggx", d), gx.at[x], gx.at[x], d_x[d])

    def gain_y():
        for d in deltas:
            got(("ggx", d))
        gy[y] = (gx[0] + gx[1]) + (gx[2] + gx[3])
        for d in deltas:
            send(("ggy", d), gy.at[y], gy.at[y], d_y[d])

    def gain_z():
        for d in deltas:
            got(("ggy", d))
        gz[z] = (gy[0] + gy[1]) + (gy[2] + gy[3])
        for d in range(1, 8):
            send(("ggz", d), gz.at[z], gz.at[z], d_z[d])

    def gain_last():
        for d in range(1, 8):
            got(("ggz", d))
        total = gz[0]
        for i in range(1, 8):
            total += gz[i]
        gg_ref[mine, :] = total
        send("gg", gg_ref.at[mine], gg_ref.at[mine], d_core)

    for i, fn in enumerate((gain_core, gain_x, gain_y, gain_z, gain_last)):
        piece(("g", i), fn)
    piece(("g", 5), got, "gg")

    for name in ORDER:
        events.pop(name)()
    assert not events and not waits
    for copy in sent:
        copy.wait_send()
    for copy in stores:
        copy.wait()


MESSAGES = 310


def on_device(
    tokens, norm_gain, value_weight, value_grads, new_logprobs, old_logprobs, advantages, lengths
):
    vmem = pl.BlockSpec(memory_space=pltpu.VMEM)
    smem = pl.BlockSpec(memory_space=pltpu.SMEM)
    hbm = pl.BlockSpec(memory_space=pl.ANY)
    input_grads, weight_grads, gain_grads = pl.pallas_call(
        kernel,
        out_shape=(
            jax.ShapeDtypeStruct((256, 8192), BF16),
            jax.ShapeDtypeStruct((512, 512), F32),
            jax.ShapeDtypeStruct((64, 128), F32),
        ),
        in_specs=[hbm, vmem, hbm, vmem, vmem, vmem, smem, smem],
        out_specs=(hbm, vmem, vmem),
        scratch_shapes=[
            pltpu.VMEM((256, 8192), BF16),
            pltpu.VMEM((16, 2, 256, 512), BF16),
            pltpu.VMEM((32, 256, 256), F32),
            pltpu.VMEM((16, 256, 256), BF16),
            pltpu.VMEM((16, 256, 256), BF16),
            pltpu.VMEM((16, 256, 256), BF16),
            pltpu.VMEM((256, 512), BF16),
            pltpu.VMEM((512, 256), BF16),
            pltpu.VMEM((512, 256), BF16),
            pltpu.VMEM((256, 128), F32),
            pltpu.VMEM((256, 128), F32),
            pltpu.VMEM((K, 4, 4, 4, R, 256), BF16),
            pltpu.VMEM((2, K, 2, 4, R, 256), BF16),
            pltpu.VMEM((2, K, 2, 4, R, 256), BF16),
            pltpu.VMEM((2, K, 2, 4, R, 256), BF16),
            pltpu.VMEM((K, 3, 4, R, 256), BF16),
            pltpu.VMEM((K, 2, 4, R, 128), BF16),
            pltpu.VMEM((K, 7, R, 128), BF16),
            pltpu.VMEM((K, 2, 2, 4, R, 128), BF16),
            pltpu.VMEM((max(len(YF), 1), 3, 4, 4, R, 256), BF16),
            pltpu.VMEM((max(len(YF), 1), 3, 4, R, 256), BF16),
            pltpu.VMEM((max(FAST, 1), 4, R, 256), BF16),
            pltpu.VMEM((max(FAST, 1), 8, R, 256), BF16),
            pltpu.VMEM((64, 128), F32),
            pltpu.VMEM((64, 128), F32),
            pltpu.VMEM((4, 32, 128), F32),
            pltpu.VMEM((4, 32, 128), F32),
            pltpu.VMEM((8, 32, 128), F32),
            pltpu.SemaphoreType.DMA((9,)),
            pltpu.SemaphoreType.DMA((MESSAGES,)),
            pltpu.SemaphoreType.DMA((MESSAGES,)),
        ],
        compiler_params=pltpu.CompilerParams(
            collective_id=0, has_side_effects=True, vmem_limit_bytes=54 * 2**20
        ),
    )(
        tokens,
        norm_gain.reshape(64, 128),
        value_weight.reshape(2, 256, 512),
        value_grads,
        new_logprobs.reshape(2, SEQ),
        old_logprobs.reshape(2, SEQ),
        advantages,
        lengths,
    )
    return input_grads, weight_grads, gain_grads.reshape(8192)


def solution(mesh):
    rows = P(("node", "dp"))
    in_specs = (
        P(("node", "dp"), None), P(), P("dp", None), P(("node", "dp"), None), rows, rows, rows, rows,
    )
    out_specs = (P(("node", "dp"), None), P("dp", None), P())
    return jax.shard_map(
        on_device, mesh=mesh, in_specs=in_specs, out_specs=out_specs, check_vma=False
    )
```

```python
import functools

import jax
import jax.numpy as jnp
from jax import lax
from jax.experimental import pallas as pl
from jax.experimental.pallas import tpu as pltpu
from jax.sharding import PartitionSpec as P

SEQ = 128
EPS = 1e-06
K = 8
R = 128 // K
YF = (7,)
FAST = 2
CUT = 192
ORDER = (
    ("t0", 0, 0), ("t0", 0, 1), ("t0", 4, "b"), ("p", 0, 0), ("xg", 0), ("p", 0, 1), ("xg", 1), ("p", 0, 2),
    ("xg", 2), ("p", 0, 3), ("xg", 3), ("t1", 0, 0), ("t0", 1, 0), ("t0", 2, 0), ("xf", 1), ("xf", 2),
    ("xf", 3), ("p", 1, 0), ("p", 1, 1), ("p", 1, 2), ("t1", 0, 1), ("p", 1, 3), ("xr", 0, 0), ("xr", 1, 0),
    ("t0", 3, 0), ("t1", 4, "b"), ("yf", 7), ("t0", 1, 1), ("t0", 2, 1), ("xr", 0, 1), ("xr", 1, 1),
    ("t2", 0, 0), ("xf", 4), ("t1", 1, 0), ("t0", 3, 1), ("t2", 0, 1), ("xr", 0, 2), ("xr", 1, 2),
    ("t1", 2, 0), ("xf", 5), ("t2", 4, "b"), ("b", 0), ("t1", 3, 0), ("xr", 0, 3), ("xr", 1, 3), ("t2", 1, 0),
    ("xf", 6), ("t1", 1, 1), ("b", 1), ("t2", 2, 0), ("xl", 0), ("t1", 2, 1), ("xl", 1), ("t2", 3, 0),
    ("xr", 0, 4), ("xr", 1, 4), ("t1", 3, 1), ("t2", 1, 1), ("ym", 7), ("t3", 0), ("xl", 2), ("t3", 4),
    ("t2", 2, 1), ("xr", 0, 5), ("xr", 1, 5), ("b", 2), ("t2", 3, 1), ("t3", 1), ("yl", 0), ("xl", 3),
    ("t4", 0), ("yl", 1), ("t4", 4), ("t3", 2), ("xr", 0, 6), ("xr", 1, 6), ("rg", 0), ("t3", 3), ("b", 3),
    ("t4", 1), ("xl", 4), ("yl", 2), ("yl", 3), ("xd", 7), ("b", 4), ("xl", 5), ("t4", 2), ("rg", 1),
    ("rg", 2), ("t4", 3), ("xl", 6), ("yl", 4), ("rg", 3), ("g", 0), ("yl", 5), ("g", 1), ("zl", 0),
    ("zl", 1), ("zl", 2), ("yl", 6), ("zl", 3), ("zl", 4), ("g", 2), ("ns", 0), ("zl", 7), ("ns", 1),
    ("zl", 5), ("ns", 2), ("fr", 0), ("fr", 1), ("ns", 3), ("fr", 2), ("ns", 4), ("fr", 3), ("g", 3),
    ("zl", 6), ("ns", 5), ("wr", 0), ("wr", 1), ("wr", 2), ("wr", 3), ("wr", 4), ("g", 4), ("wr", 5),
    ("wr", 6), ("wr", 7), ("g", 5),
)
MESH = pl.DeviceIdType.MESH
F32 = jnp.float32
BF16 = jnp.bfloat16


def mod(a, n):
    return lax.rem(a + 2 * n, n)


def kernel(
    tok_hbm, gain_ref, w_hbm, vg_ref, new_ref, old_ref, adv_ref, len_ref,
    ig_hbm, wg_ref, gg_ref,
    tok, wfull, ngs, nown, nsend, nrecv, cot, cot_t, cot_t_in, inv_ref, acc,
    part, xin_a, xin_b, xin_c, yin, ts, zin, wt, yf_in, xd_in, tsf, zinf,
    gpart, gcore, gx, gy, gz,
    lsem, ssem, rsem,
):
    node = lax.axis_index("node")
    dp = lax.axis_index("dp")
    c = lax.rem(node, 2)
    x = lax.rem(node // 2, 4)
    lo = node // 8
    h = dp // 4
    y = lax.rem(dp, 4)
    z = 2 * h + lo
    j_me = dp

    def dev(x=x, y=y, z=z, c=c):
        return (lax.rem(z, 2) * 8 + x * 2 + c, (z // 2) * 4 + y)

    sgn = 2 * lo - 1
    z_out = mod(z + sgn, 8)
    z_mate = mod(z - sgn, 8)
    d_core = dev(c=1 - c)
    d_x = {1: dev(x=mod(x + 1, 4)), -1: dev(x=mod(x - 1, 4)), 2: dev(x=mod(x + 2, 4))}
    d_y = {1: dev(y=mod(y + 1, 4)), -1: dev(y=mod(y - 1, 4)), 2: dev(y=mod(y + 2, 4))}
    d_out = dev(z=z_out)
    d_mate = dev(z=z_mate)
    d_z = {d: dev(z=mod(z + d, 8)) for d in range(1, 8)}

    d_diag = dev(z=z_mate, c=1 - c)
    d_xf = {d: dev(x=mod(x + d, 4), c=1 - c) for d in (1, -1, 2)}

    barrier = pltpu.get_barrier_semaphore()
    peers = [d_core, *d_x.values(), *d_xf.values(), *d_y.values(), *d_z.values(), d_diag]
    for peer in peers:
        pl.semaphore_signal(barrier, inc=1, device_id=peer, device_id_type=MESH)

    loads = []
    for r in range(4):
        loads.append(pltpu.make_async_copy(
            tok_hbm.at[pl.ds(r * 64, 64)], tok.at[pl.ds(r * 64, 64)], lsem.at[r]))
    wload = pltpu.make_async_copy(w_hbm, wfull.at[j_me], lsem.at[4])
    for cp in loads:
        cp.start()
    wload.start()

    names = {}
    sent = []

    def message(name, src, dst, device):
        index = names.setdefault(name, len(names))
        return pltpu.make_async_remote_copy(
            src_ref=src, dst_ref=dst, send_sem=ssem.at[index], recv_sem=rsem.at[index],
            device_id=device, device_id_type=MESH)

    waits = {}

    def send(name, src, dst, device):
        copy = message(name, src, dst, device)
        copy.start()
        sent.append(copy)
        waits[name] = copy

    def got(name):
        waits.pop(name).wait_recv()

    row = lax.broadcasted_iota(jnp.int32, (2, SEQ), 0)
    pos = lax.broadcasted_iota(jnp.int32, (2, SEQ), 1)
    adv = jnp.where(row == 0, adv_ref[0], adv_ref[1])
    length = jnp.where(row == 0, len_ref[0], len_ref[1])
    alive = (pos < length).astype(F32)
    ratio = jnp.exp(new_ref[...] - old_ref[...])
    weight = -adv * jnp.clip(ratio, 0.8, 1.2) / SEQ * alive
    eye = lax.broadcasted_iota(jnp.int32, (SEQ, SEQ), 0) == lax.broadcasted_iota(
        jnp.int32, (SEQ, SEQ), 1)
    for s in range(2):
        column = jnp.sum(jnp.where(eye, weight[s : s + 1, :], 0.0), axis=1, keepdims=True)
        wide = column * vg_ref[pl.ds(s * SEQ, SEQ), :].astype(F32)
        cot[pl.ds(s * SEQ, SEQ), :] = wide.astype(BF16)
        cot_t[:, pl.ds(s * SEQ, SEQ)] = wide.T.astype(BF16)

    for r in range(4):
        loads[r].wait()
        rows = pl.ds(r * 64, 64)

        def squares(i, total):
            part_ = tok[rows, pl.ds(pl.multiple_of(i * 512, 512), 512)].astype(F32)
            part_ = part_ * part_
            return total + ((part_[:, :128] + part_[:, 128:256])
                            + (part_[:, 256:384] + part_[:, 384:]))

        total = lax.fori_loop(0, 16, squares, jnp.zeros((64, 128), F32), unroll=2)
        mean = jnp.sum(total, axis=1, keepdims=True) / 8192.0
        inv_ref[rows, :] = jnp.broadcast_to(lax.rsqrt(mean + EPS), (64, 128))

    def inverse():
        return inv_ref[:, 0:1]

    def gain_row(block):
        return jnp.concatenate([gain_ref[pl.ds(2 * block, 1), :], gain_ref[pl.ds(2 * block + 1, 1), :]], axis=1)

    def norm_block(block, dst, jj):
        lanes = pl.ds(pl.multiple_of(block * 256, 256), 256)
        value = tok[:, lanes].astype(F32) * inverse() * gain_row(block)
        dst[jj] = value.astype(BF16)

    @pl.loop(0, 16)
    def _(jj):
        norm_block(2 * jj + (1 - c), nsend, jj)

    @pl.loop(0, 16)
    def _(jj):
        norm_block(2 * jj + c, nown, jj)

    wload.wait()
    pl.semaphore_wait(barrier, len(peers))

    events = {}

    def piece(name, fn, *args):
        events[name] = functools.partial(fn, *args)

    send("cot", cot_t, cot_t_in, d_core)
    for g in range(4):
        send(("n", g), nsend.at[pl.ds(4 * g, 4)], nrecv.at[pl.ds(4 * g, 4)], d_core)

    deltas = (1, -1, 2)

    from_core = {0: [], 1: [], 2: [], 3: []}

    def to_core(name, ref, group):
        send(("k", name), ref, ref, d_core)
        from_core[group].append(("k", name))

    def rows_of(unit):
        if unit[1] == "b":
            return CUT, 256 - CUT
        return unit[1] * (CUT // 2), CUT // 2

    def half_rows(u, which):
        if u == 4:
            return CUT + which * ((256 - CUT) // 2), (256 - CUT) // 2
        return which * (CUT // 2), CUT // 2

    def y_of(u):
        return y + (0, -1, 1, 2, 0)[u]

    def block_rows(hh, yy, base, count):
        return wfull.at[mod(hh, 4) * 4 + mod(yy, 4), c, pl.ds(pl.multiple_of(base, 16), count)]

    def group_of(u):
        return u % 4

    def spread_b(tag, hh, base, count):
        ref = block_rows(hh, y, base, count)
        for d in deltas:
            send(("by", tag, d), ref, ref, d_y[d])

    def got_b(tag, hh, base, count):
        for i, d in enumerate(deltas):
            got(("by", tag, d))
            to_core(("by", tag, d), block_rows(hh, y - d, base, count), i + 1)

    def t0(unit):
        u, s = unit
        base, count = rows_of(unit)
        if u in (1, 2, 3):
            d = deltas[u - 1]
            got(("ay", d, s))
            to_core(("ay", d, s), block_rows(h, y - d, base, count), u)
        ref = block_rows(h, y_of(u), base, count)
        send(("o1", unit), ref, ref, d_out)
        if u == 4:
            spread_b("own", h, base, count)
        elif u == 0:
            for d in deltas:
                send(("ay", d, s), ref, ref, d_y[d])

    def t1(unit):
        u = unit[0]
        base, count = rows_of(unit)
        got(("o1", unit))
        ref = block_rows(h + sgn, y_of(u), base, count)
        send(("m1", unit), ref, ref, d_mate)
        to_core(("o1", unit), ref, group_of(u))
        if u == 4:
            spread_b("out", h + sgn, base, count)

    def t2(unit):
        u, s = unit
        base, count = rows_of(unit)
        got(("m1", unit))
        ref = block_rows(h - sgn, y_of(u), base, count)
        if s != 0:
            half = block_rows(h - sgn, y_of(u), *half_rows(u, 1 - lo))
            send(("o2", u), half, half, d_out)
        to_core(("m1", unit), ref, group_of(u))
        if u == 4:
            spread_b("mate", h - sgn, base, count)

    def t3(u):
        got(("o2", u))
        first, size = half_rows(u, lo)
        ref = block_rows(h + 2, y_of(u), first, size)
        send(("m2", u), ref, ref, d_mate)
        to_core(("o2", u), ref, group_of(u))
        if u == 4:
            spread_b("far1", h + 2, first, size)

    def t4(u):
        got(("m2", u))
        first, size = half_rows(u, 1 - lo)
        ref = block_rows(h + 2, y_of(u), first, size)
        to_core(("m2", u), ref, group_of(u))
        if u == 4:
            spread_b("far2", h + 2, first, size)

    for u in range(5):
        for s in ((0, 1) if u < 4 else ("b",)):
            piece(("t0", u, s), t0, (u, s))
            piece(("t1", u, s), t1, (u, s))
            piece(("t2", u, s), t2, (u, s))
        piece(("t3", u), t3, u)
        piece(("t4", u), t4, u)
    b_rows = rows_of((4, "b"))
    piece(("b", 0), got_b, "own", h, *b_rows)
    piece(("b", 1), got_b, "out", h + sgn, *b_rows)
    piece(("b", 2), got_b, "mate", h - sgn, *b_rows)
    piece(("b", 3), got_b, "far1", h + 2, *half_rows(4, lo))
    piece(("b", 4), got_b, "far2", h + 2, *half_rows(4, 1 - lo))

    M = 256
    chunk_rows = 4 * R

    def products(m, g):
        if (m, g) == (0, 0):
            got("cot")
        if m == 0:
            got(("n", g))

        @pl.loop(0, 4, unroll=4)
        def _(yy):
            jj = 4 * g + yy
            rows = pl.ds(m * M, M)
            value = jnp.dot(cot_t[rows, :], nown[jj], preferred_element_type=F32)
            value += jnp.dot(cot_t_in[rows, :], nrecv[jj], preferred_element_type=F32)
            value = value.astype(BF16)
            for k in range(M // chunk_rows):
                for q in range(4):
                    first = k * chunk_rows + q * R
                    part[m * (M // chunk_rows) + k, q, yy, g] = value[first : first + R]

    for m in range(2):
        for g in range(4):
            piece(("p", m, g), products, m, g)

    first_half, second_half = pl.ds(0, 2), pl.ds(2, 2)

    def x_first(k):
        x2, xr, xl = mod(x + 2, 4), mod(x + 1, 4), mod(x - 1, 4)
        send(("xa", 0, k), part.at[k, x2, first_half], xin_a.at[0, k], d_x[1])
        send(("xa", 1, k), part.at[k, x2, second_half], xin_a.at[1, k], d_x[-1])
        send(("xb", 0, k), part.at[k, xr, second_half], xin_b.at[0, k], d_x[1])
        send(("xb", 1, k), part.at[k, xl, first_half], xin_b.at[1, k], d_x[-1])

    def x_early(g):
        x2, xr, xl = mod(x + 2, 4), mod(x + 1, 4), mod(x - 1, 4)
        for kind, way, q, half, into in (
            ("xa", 0, x2, first_half, xin_a), ("xa", 1, x2, second_half, xin_a),
            ("xb", 0, xr, second_half, xin_b), ("xb", 1, xl, first_half, xin_b),
        ):
            send((kind, way, 0, g), part.at[0, q, half, g], into.at[way, 0, pl.ds(0, 2), g],
                 d_x[(1, -1)[way]])

    def got_x(kind, way, k):
        if k == 0:
            for g in range(4):
                got((kind, way, 0, g))
        else:
            got((kind, way, k))

    def add_into(k, q, half, *others):
        @pl.loop(0, 2, unroll=2)
        def _(i):
            value = part[k, q, half * 2 + i].astype(F32)
            for other in others:
                value += other[i].astype(F32)
            part[k, q, half * 2 + i] = value.astype(BF16)

    def x_relay(way, k):
        q = mod(x + (1, -1)[way], 4)
        got_x("xa", way, k)
        add_into(k, q, way, xin_a.at[way, k])
        half = (first_half, second_half)[way]
        send(("xc", way, k), part.at[k, q, half], xin_c.at[way, k], d_x[(1, -1)[way]])

    def x_last(k):
        for way in range(2):
            got_x("xb", 1 - way, k)
            got(("xc", way, k))
            add_into(k, x, way, xin_c.at[way, k], xin_b.at[1 - way, k])
        for i, d in enumerate(deltas):
            send(("y", d, k), part.at[k, x, mod(y + d, 4)], yin.at[k, i], d_y[d])

    def y_last(k):
        for d in deltas:
            got(("y", d, k))
        value = part[k, x, y].astype(F32)
        for i in range(3):
            value += yin[k, i].astype(F32)
        z_first(k, value.astype(BF16))

    def z_first(k, value):
        fast = k - (K - FAST)
        if fast >= 0:
            tsf[fast] = value
            zinf[fast, z] = tsf[fast, h]
            for d in range(1, 8):
                send(("z", d, k), tsf.at[fast, mod(z + d, 8) // 2], zinf.at[fast, z], d_z[d])
            return
        ts[k, 0] = value[:, :, :128]
        ts[k, 1] = value[:, :, 128:]
        for d in range(1, 8):
            z_to = mod(z + d, 8)
            send(("z", d, k), ts.at[k, lax.rem(z_to, 2), z_to // 2], zin.at[k, d - 1], d_z[d])

    def y_first(k):
        n = YF.index(k)
        for i, d in enumerate(deltas):
            send(("yf", d, k), part.at[k, pl.ds(0, 4), mod(y + d, 4)], yf_in.at[n, i], d_y[d])

    def y_middle(k):
        n = YF.index(k)
        for d in deltas:
            got(("yf", d, k))

        @pl.loop(0, 4)
        def _(q):
            value = part[k, q, y].astype(F32)
            for i in range(3):
                value += yf_in[n, i, q].astype(F32)
            part[k, q, y] = value.astype(BF16)

        for i, d in enumerate(deltas):
            send(("xd", d, k), part.at[k, mod(x + d, 4), y], xd_in.at[n, i], d_x[d])

    def x_direct_last(k):
        n = YF.index(k)
        for d in deltas:
            got(("xd", d, k))
        value = part[k, x, y].astype(F32)
        for i in range(3):
            value += xd_in[n, i].astype(F32)
        z_first(k, value.astype(BF16))

    def z_last(k):
        for d in range(1, 8):
            got(("z", d, k))
        fast = k - (K - FAST)
        if fast >= 0:
            value = zinf[fast, 0].astype(F32)
            for i in range(1, 8):
                value += zinf[fast, i].astype(F32)
            value = value.astype(BF16)
            wt[k, c, 0, x] = value[:, :128]
            wt[k, c, 1, x] = value[:, 128:]
            ref = wt.at[k, c, pl.ds(0, 2), x]
            send(("gf", 0, k), ref, ref, d_core)
            for d in deltas:
                send(("gf", d, k), ref, ref, d_x[d])
                send(("gg", d, k), ref, ref, d_xf[d])
            return
        value = ts[k, lo, h].astype(F32)
        for d in range(7):
            value += zin[k, d].astype(F32)
        wt[k, c, lo, x] = value.astype(BF16)
        ref = wt.at[k, c, lo, x]
        for d in deltas:
            send(("gx", d, k), ref, ref, d_x[d])

    def node_share(k):
        for d in deltas:
            got(("gx", d, k))
        ref = wt.at[k, c, lo]
        send(("gc", k), ref, ref, d_core)
        send(("gm", k), ref, ref, d_mate)
        send(("gd", k), ref, ref, d_diag)

    def write_block(k):
        if k >= K - FAST:
            got(("gf", 0, k))
            for d in deltas:
                got(("gf", d, k))
                got(("gg", d, k))
        else:
            for n in ("gc", "gm", "gd"):
                got((n, k))
        if (k + 1) * chunk_rows % SEQ == 0:
            first = (k + 1) * chunk_rows // SEQ - 1
            count = SEQ // chunk_rows
            for cc in range(2):
                for ll in range(2):
                    value = wt[pl.ds(first * count, count), cc, ll].astype(F32)
                    value = value.reshape(SEQ, 128)
                    wg_ref[pl.ds(cc * 256 + ll * 128, 128), pl.ds(first * SEQ, SEQ)] = value.T

    for k in range(K):
        if k in YF:
            piece(("yf", k), y_first, k)
            piece(("ym", k), y_middle, k)
            piece(("xd", k), x_direct_last, k)
        else:
            if k == 0:
                for g in range(4):
                    piece(("xg", g), x_early, g)
            else:
                piece(("xf", k), x_first, k)
            piece(("xr", 0, k), x_relay, 0, k)
            piece(("xr", 1, k), x_relay, 1, k)
            piece(("xl", k), x_last, k)
            piece(("yl", k), y_last, k)
        piece(("zl", k), z_last, k)
        if k < K - FAST:
            piece(("ns", k), node_share, k)
        piece(("wr", k), write_block, k)

    acc[...] = jnp.zeros_like(acc)

    def row_grads(group):
        for name in from_core[group]:
            got(name)
        yb = mod(y_of(group), 4)

        @pl.loop(0, 8, unroll=4)
        def _(i):
            block = ((i // 2) * 4 + yb) * 2 + lax.rem(i, 2)
            lanes = pl.ds(pl.multiple_of(block * 256, 256), 256)
            ng = lax.dot_general(
                cot[...], wfull[(i // 2) * 4 + yb, lax.rem(i, 2)], (((1,), (1,)), ((), ())),
                preferred_element_type=F32)
            ngs[block] = ng
            both = ng * tok[:, lanes].astype(F32)
            sums = jnp.sum(both * inverse(), axis=0, keepdims=True)
            gpart[pl.ds(2 * block, 1), :] = sums[:, :128]
            gpart[pl.ds(2 * block + 1, 1), :] = sums[:, 128:]
            both = both * gain_row(block)
            acc[...] += both[:, :128] + both[:, 128:]

    for group in range(4):
        piece(("rg", group), row_grads, group)

    stores = []

    def finish_rows(quarter):
        inv = inverse()
        coef = inv * inv * inv * (jnp.sum(acc[...], axis=1, keepdims=True) / 8192.0)

        @pl.loop(0, 8, unroll=2)
        def _(i):
            block = quarter * 8 + i
            lanes = pl.ds(pl.multiple_of(block * 256, 256), 256)
            value = inv * (gain_row(block) * ngs[block]) - tok[:, lanes].astype(F32) * coef
            tok[:, lanes] = value.astype(BF16)

        lanes = pl.ds(quarter * 2048, 2048)
        copy = pltpu.make_async_copy(tok.at[:, lanes], ig_hbm.at[:, lanes], lsem.at[5 + quarter])
        copy.start()
        stores.append(copy)

    for quarter in range(4):
        piece(("fr", quarter), finish_rows, quarter)

    mine = pl.ds(pl.multiple_of(32 * c, 32), 32)

    def gain_core():
        send("g", gpart, gcore, d_core)

    def gain_x():
        got("g")
        gx[x] = gpart[mine, :] + gcore[mine, :]
        for d in deltas:
            send(("ggx", d), gx.at[x], gx.at[x], d_x[d])

    def gain_y():
        for d in deltas:
            got(("ggx", d))
        gy[y] = (gx[0] + gx[1]) + (gx[2] + gx[3])
        for d in deltas:
            send(("ggy", d), gy.at[y], gy.at[y], d_y[d])

    def gain_z():
        for d in deltas:
            got(("ggy", d))
        gz[z] = (gy[0] + gy[1]) + (gy[2] + gy[3])
        for d in range(1, 8):
            send(("ggz", d), gz.at[z], gz.at[z], d_z[d])

    def gain_last():
        for d in range(1, 8):
            got(("ggz", d))
        total = gz[0]
        for i in range(1, 8):
            total += gz[i]
        gg_ref[mine, :] = total
        send("gg", gg_ref.at[mine], gg_ref.at[mine], d_core)

    for i, fn in enumerate((gain_core, gain_x, gain_y, gain_z, gain_last)):
        piece(("g", i), fn)
    piece(("g", 5), got, "gg")

    for name in ORDER:
        events.pop(name)()
    assert not events and not waits
    for copy in sent:
        copy.wait_send()
    for copy in stores:
        copy.wait()


MESSAGES = 305


def on_device(
    tokens, norm_gain, value_weight, value_grads, new_logprobs, old_logprobs, advantages, lengths
):
    vmem = pl.BlockSpec(memory_space=pltpu.VMEM)
    smem = pl.BlockSpec(memory_space=pltpu.SMEM)
    hbm = pl.BlockSpec(memory_space=pl.ANY)
    input_grads, weight_grads, gain_grads = pl.pallas_call(
        kernel,
        out_shape=(
            jax.ShapeDtypeStruct((256, 8192), BF16),
            jax.ShapeDtypeStruct((512, 512), F32),
            jax.ShapeDtypeStruct((64, 128), F32),
        ),
        in_specs=[hbm, vmem, hbm, vmem, vmem, vmem, smem, smem],
        out_specs=(hbm, vmem, vmem),
        scratch_shapes=[
            pltpu.VMEM((256, 8192), BF16),
            pltpu.VMEM((16, 2, 256, 512), BF16),
            pltpu.VMEM((32, 256, 256), F32),
            pltpu.VMEM((16, 256, 256), BF16),
            pltpu.VMEM((16, 256, 256), BF16),
            pltpu.VMEM((16, 256, 256), BF16),
            pltpu.VMEM((256, 512), BF16),
            pltpu.VMEM((512, 256), BF16),
            pltpu.VMEM((512, 256), BF16),
            pltpu.VMEM((256, 128), F32),
            pltpu.VMEM((256, 128), F32),
            pltpu.VMEM((K, 4, 4, 4, R, 256), BF16),
            pltpu.VMEM((2, K, 2, 4, R, 256), BF16),
            pltpu.VMEM((2, K, 2, 4, R, 256), BF16),
            pltpu.VMEM((2, K, 2, 4, R, 256), BF16),
            pltpu.VMEM((K, 3, 4, R, 256), BF16),
            pltpu.VMEM((K, 2, 4, R, 128), BF16),
            pltpu.VMEM((K, 7, R, 128), BF16),
            pltpu.VMEM((K, 2, 2, 4, R, 128), BF16),
            pltpu.VMEM((max(len(YF), 1), 3, 4, 4, R, 256), BF16),
            pltpu.VMEM((max(len(YF), 1), 3, 4, R, 256), BF16),
            pltpu.VMEM((max(FAST, 1), 4, R, 256), BF16),
            pltpu.VMEM((max(FAST, 1), 8, R, 256), BF16),
            pltpu.VMEM((64, 128), F32),
            pltpu.VMEM((64, 128), F32),
            pltpu.VMEM((4, 32, 128), F32),
            pltpu.VMEM((4, 32, 128), F32),
            pltpu.VMEM((8, 32, 128), F32),
            pltpu.SemaphoreType.DMA((9,)),
            pltpu.SemaphoreType.DMA((MESSAGES,)),
            pltpu.SemaphoreType.DMA((MESSAGES,)),
        ],
        compiler_params=pltpu.CompilerParams(
            collective_id=0, has_side_effects=True, vmem_limit_bytes=54 * 2**20
        ),
    )(
        tokens,
        norm_gain.reshape(64, 128),
        value_weight.reshape(2, 256, 512),
        value_grads,
        new_logprobs.reshape(2, SEQ),
        old_logprobs.reshape(2, SEQ),
        advantages,
        lengths,
    )
    return input_grads, weight_grads, gain_grads.reshape(8192)


def solution(mesh):
    rows = P(("node", "dp"))
    in_specs = (
        P(("node", "dp"), None), P(), P("dp", None), P(("node", "dp"), None), rows, rows, rows, rows,
    )
    out_specs = (P(("node", "dp"), None), P("dp", None), P())
    return jax.shard_map(
        on_device, mesh=mesh, in_specs=in_specs, out_specs=out_specs, check_vma=False
    )
```
